512 devices in a mesh: dp: 16 (over y, core), worker: 32 (over x, z).
Axes of the slice: x: 4, y: 8, z: 8, core: 2. Of those that a mesh axis runs over, the one named last changes fastest.
Arguments:
- grad: bfloat16 [48, 32, 512, 512], P('dp', 'worker')
- prev_stats: float32 [32, 2, 512, 512], P('worker', None, 'dp')
- warm_roots: float32 [32, 2, 512, 512], P('worker', None, 'dp')
- owner_items: int32 [32, 2], replicated, may hold values from 0 to 63, as said below
- counts: int32 [64], replicated, may hold values from 1 to 2, as said below
- read_shard: int32 [32], replicated, may hold values from 0 to 31, each once
Outputs:
- roots: float32 [32, 2, 512, 512], P('worker', None, 'dp')
The draws below stay inside these ranges and needn't reach their ends.
Inputs may be any that keep to these rules, and one draw needn't show every extreme that they name: `owner_items`: each of the 64 statistics stands in exactly one slot; the counts of an owner's two statistics sum to at most 3, and some owner's sum to 3. `counts`: every owner holds one statistic of count 1 and one of count 1 or 2. `read_shard`: each shard reads exactly one block.
All inputs are finite; a program needn't handle non-finite values.
Results may differ from the reference program's by a relative error of at most 0.0003.
Values sent between devices are 32-bit elements; how exact they have to be, the bound alone decides.
No kernel may reach another device: no remote copies, remote signals or barrier semaphores. Data moves between devices by JAX's collectives and lax.ppermute only.
A program may use at most 64 MiB of HBM per device.

```python
import math
import jax
import jax.numpy as jnp
from jax import lax

B = 512
MB = 3
REPLICAS = 16
GRADS = 48
NBLK = 32
FACT = 64


COMMON = 0.5


def owner_plan(key):
    order = jax.random.permutation(jax.random.fold_in(key, 11), FACT).astype(jnp.int32)
    second = jax.random.randint(jax.random.fold_in(key, 12), (NBLK,), 1, 3).astype(jnp.int32)
    forced = jax.random.randint(jax.random.fold_in(key, 13), (), 0, NBLK)
    second = jnp.where(jnp.arange(NBLK) == forced, 2, second).astype(jnp.int32)
    flips = jax.random.randint(jax.random.fold_in(key, 14), (NBLK, 1), 0, 2)
    pairs = order.reshape(NBLK, 2)
    slot_counts = jnp.stack([jnp.ones((NBLK,), jnp.int32), second], 1)
    pairs = jnp.where(flips == 1, pairs[:, ::-1], pairs)
    slot_counts = jnp.where(flips == 1, slot_counts[:, ::-1], slot_counts)
    return (pairs.astype(jnp.int32), slot_counts.astype(jnp.int32))


def block_levels(key):
    prev_level = jax.random.uniform(jax.random.fold_in(key, 51), (NBLK, 2, B), minval=0.0, maxval=math.log(10.0))
    column_level = jax.random.uniform(jax.random.fold_in(key, 52), (NBLK, B), minval=0.0, maxval=math.log(10.0))
    row_level = jax.random.uniform(jax.random.fold_in(key, 53), (NBLK, B), minval=0.0, maxval=math.log(3.0))
    return (prev_level, column_level, row_level)


def draw_owner_items(key, part):
    pairs, slot_counts = owner_plan(key)
    return pairs


def draw_counts(key, part):
    pairs, slot_counts = owner_plan(key)
    return jnp.zeros((FACT,), jnp.int32).at[pairs.reshape(-1)].set(slot_counts.reshape(-1))


def draw_grad(key, part):
    prev_level, column_level, row_level = block_levels(key)
    key = jax.random.fold_in(key, 21)
    noise_key, shared_key = jax.random.split(key)
    rise = jnp.sqrt(1.0 + 2.0 * (jnp.arange(GRADS) // MB).astype(jnp.float32) / max(REPLICAS - 1, 1))
    column_scale = jnp.exp(0.5 * column_level)[None, :, None, :]
    row_scale = jnp.exp(0.5 * row_level)[None, :, :, None]
    noise = jax.random.normal(noise_key, (GRADS, NBLK, B, B))
    shared = jax.random.normal(shared_key, (1, NBLK, B, B))
    base = math.sqrt(1.0 - COMMON) * noise + math.sqrt(COMMON) * shared
    return (base * row_scale * column_scale * rise[:, None, None, None]).astype(jnp.bfloat16)


def draw_prev_stats(key, part):
    prev_level, column_level, row_level = block_levels(key)
    key = jax.random.fold_in(key, 31)
    diagonal = B * jnp.exp(prev_level)
    noise = jax.random.uniform(key, (NBLK, 2, B, B), minval=-1.0, maxval=1.0)
    identity = jnp.eye(B, dtype=jnp.float32)
    offdiag = (noise + jnp.swapaxes(noise, -1, -2)) * 0.1
    return offdiag * (1.0 - identity) + diagonal[..., None] * identity


def draw_warm_roots(key, part):
    prev_level, column_level, row_level = block_levels(key)
    key = jax.random.fold_in(key, 41)
    first_key, second_key = jax.random.split(key)
    left_level = B * (9.0 / math.log(10.0)) * jnp.exp(row_level)
    right_level = B * (2.0 / math.log(3.0)) * jnp.exp(column_level)
    expected = 0.5 * B * jnp.exp(prev_level) + jnp.stack([left_level, right_level], 1)
    frobenius = jnp.sqrt(jnp.array([108.0, 120.0], jnp.float32) * float(B) ** 3)
    target = (expected / frobenius[None, :, None]) ** (-0.25)
    factor = jax.random.uniform(first_key, (NBLK, 2, B), minval=0.85, maxval=1.15)
    diagonal = target * factor
    noise = jax.random.uniform(second_key, (NBLK, 2, B, B), minval=-1.0, maxval=1.0)
    identity = jnp.eye(B, dtype=jnp.float32)
    offdiag = (noise + jnp.swapaxes(noise, -1, -2)) * (0.12 / B)
    return offdiag * (1.0 - identity) + diagonal[..., None] * identity


def setup_inputs(seed: int = 0) -> dict:
    key_list = jax.random.split(jax.random.key(seed), 7)
    return {
        "grad": draw_grad(jax.random.fold_in(key_list[6], 71), 0),
        "prev_stats": draw_prev_stats(jax.random.fold_in(key_list[6], 71), 0),
        "warm_roots": draw_warm_roots(jax.random.fold_in(key_list[6], 71), 0),
        "owner_items": draw_owner_items(jax.random.fold_in(key_list[6], 71), 0),
        "counts": draw_counts(jax.random.fold_in(key_list[6], 71), 0),
        "read_shard": jax.random.permutation(key_list[5], NBLK).astype(jnp.int32),
    }


HISTORY = 0.5
DAMPING = 0.001
PRECISE = lax.Precision.HIGHEST

def precise_dot(first, second):
    return jnp.dot(first, second, precision=PRECISE, preferred_element_type=jnp.float32)

def block_stats(index, grad, prev_stats):
    gradients = lax.dynamic_index_in_dim(grad, index, 1, keepdims=False).astype(jnp.float32)
    left_part = jnp.einsum('mik,mjk->ij', gradients, gradients, precision=PRECISE)
    right_part = jnp.einsum('mki,mkj->ij', gradients, gradients, precision=PRECISE)
    previous = lax.dynamic_index_in_dim(prev_stats, index, 0, keepdims=False)
    return HISTORY * previous + (1.0 - HISTORY) / GRADS * jnp.stack([left_part, right_part])

def refine(statistic, warm_start, iterations):
    frobenius = jnp.sqrt(jnp.sum(statistic * statistic) + 1e-06)
    identity = jnp.eye(B, dtype=jnp.float32)
    scaled = statistic / frobenius + DAMPING * identity
    squared = precise_dot(warm_start, warm_start)
    coupled = precise_dot(precise_dot(squared, squared), scaled)
    step_factor = (5.0 * identity - coupled) * 0.25
    estimate = precise_dot(warm_start, step_factor)
    factor_sq = precise_dot(step_factor, step_factor)
    coupled = precise_dot(factor_sq, precise_dot(factor_sq, coupled))
    step_factor = (5.0 * identity - coupled) * 0.25
    return jnp.where(iterations >= 2, precise_dot(estimate, step_factor), estimate)

def reference(grad, prev_stats, warm_roots, owner_items, counts, read_shard):
    stats = lax.map(lambda index: block_stats(index, grad, prev_stats), jnp.arange(NBLK, dtype=jnp.int32))
    flat_stats = stats.reshape(FACT, B, B)
    slot_items = owner_items.reshape(FACT).astype(jnp.int32)
    slot_warm = warm_roots.reshape(FACT, B, B)

    def one_slot(position):
        item = slot_items[position]
        statistic = lax.dynamic_index_in_dim(flat_stats, item, 0, keepdims=False)
        warm_start = lax.dynamic_index_in_dim(slot_warm, position, 0, keepdims=False)
        return refine(statistic, warm_start, counts[item])
    slot_roots = lax.map(one_slot, jnp.arange(FACT, dtype=jnp.int32))
    by_item = jnp.zeros((FACT, B, B), jnp.float32).at[slot_items].set(slot_roots)
    return jnp.zeros((NBLK, 2, B, B), jnp.float32).at[read_shard.astype(jnp.int32)].set(by_item.reshape(NBLK, 2, B, B))
```

```python
import jax
import jax.numpy as jnp
from jax import lax
from jax.experimental import pallas as pl
from jax.experimental.pallas import tpu as pltpu
from jax.sharding import Mesh, PartitionSpec as P

HISTORY = 0.5
DAMPING = 0.001
WORKER = ("x", "z")
SWAP = [(0, 1), (1, 0)]


def dot(first, second):
    return jnp.dot(
        first, second, precision=lax.Precision.HIGHEST, preferred_element_type=jnp.float32
    )


def to_tiles(rows):
    height, width = rows.shape
    tiles = rows.reshape(height // 8, 8, width // 128, 128).transpose(0, 2, 1, 3)
    return tiles.reshape(-1, 8, 128)


def from_tiles(tiles, height, width):
    split = tiles.reshape(height // 8, width // 128, 8, 128).transpose(0, 2, 1, 3)
    return split.reshape(height, width)


def pick_kernel(block_ref, owner_ref, mine_ref, stat_ref, own_ref, sibling_ref, out_ref):
    for reader in range(out_ref.shape[0]):
        owner = owner_ref[reader]
        out_ref[reader, 0] = stat_ref[block_ref[reader]]
        out_ref[reader, 1] = jnp.where(mine_ref[reader] != 0, own_ref[owner], sibling_ref[owner])


def pick(blocks, owners, mine, stat, own_slot, sibling_slot):
    smem = pl.BlockSpec(memory_space=pltpu.SMEM)
    vmem = pl.BlockSpec(memory_space=pltpu.VMEM)
    return pl.pallas_call(
        pick_kernel,
        out_shape=jax.ShapeDtypeStruct((stat.shape[0], 2) + stat.shape[1:], stat.dtype),
        in_specs=[smem, smem, smem, vmem, vmem, vmem],
        out_specs=vmem,
    )(blocks, owners, mine, stat, own_slot, sibling_slot)


def local(grad, prev_stats, warm_roots, owner_items, counts, read_shard):
    gradients = grad[:, 0]
    width = gradients.shape[-1]
    y_count = lax.axis_size("y")
    y = lax.axis_index("y")
    core = lax.axis_index("core")
    workers = lax.axis_size(WORKER)
    worker = lax.axis_index(WORKER)
    even = core == 0
    share = width // y_count
    half = share // 2
    weight = (1.0 - HISTORY) / (y_count * 2 * gradients.shape[0])

    warm = warm_roots[0]
    warm_sent = jnp.where(even, warm[1], warm[0])
    warm_kept = jnp.where(even, warm[0], warm[1])
    warm_got = lax.ppermute(warm_sent, "core", SWAP)
    own_warm = jnp.where(
        even,
        jnp.concatenate([warm_kept, warm_got], 0),
        jnp.concatenate([warm_got, warm_kept], 0),
    )

    left = jnp.einsum("mik,mjk->ij", gradients, gradients, preferred_element_type=jnp.float32)
    right = jnp.einsum("mki,mkj->ij", gradients, gradients, preferred_element_type=jnp.float32)
    row = (y * 2 + core) * half
    partial_sent = weight * jnp.where(even, right, left)
    partial_kept = weight * jnp.where(even, left, right)
    prev_sent = HISTORY * jnp.where(even, prev_stats[0, 1], prev_stats[0, 0])
    prev_kept = HISTORY * jnp.where(even, prev_stats[0, 0], prev_stats[0, 1])
    partial_got = lax.ppermute(partial_sent, "core", SWAP)
    prev_got = lax.ppermute(prev_sent, "core", SWAP)
    chip_sum = partial_kept + partial_got
    chunks = lax.all_to_all(chip_sum.reshape(y_count, share, width), "y", 0, 0, tiled=True)
    prev_rows = jnp.where(
        even,
        jnp.concatenate([prev_kept, prev_got], 0),
        jnp.concatenate([prev_got, prev_kept], 0),
    )
    stat_rows = prev_rows + jnp.sum(chunks, axis=0)

    ids = jnp.arange(workers, dtype=jnp.int32)
    blocks = jnp.sum(jnp.where(read_shard[None, :] == ids[:, None], ids[None, :], 0), 1)
    items = 2 * blocks + core
    matches = owner_items[None] == items[:, None, None]
    owners = jnp.sum(jnp.where(matches, ids[None, :, None], 0), (1, 2))
    slots = jnp.sum(jnp.where(matches, jnp.arange(2, dtype=jnp.int32), 0), (1, 2))
    mine = (slots == core).astype(jnp.int32)

    spread = jnp.stack([to_tiles(stat_rows), to_tiles(own_warm)], 1)
    spread = lax.all_to_all(spread, WORKER, 0, 0, tiled=True)
    own_slot = spread[:, 1]
    sibling_slot = lax.ppermute(own_slot, "core", SWAP)
    ordered = pick(blocks, owners, mine, spread[:, 0], own_slot, sibling_slot)
    arrived = lax.all_to_all(ordered, WORKER, 0, 0, tiled=True)
    stat_rows = from_tiles(arrived[:, 0], share, width)
    warm_rows = from_tiles(arrived[:, 1], share, width)
    warm_start = lax.all_gather(warm_rows, "y", axis=0, tiled=True)
    statistic = lax.all_gather(stat_rows, "y", axis=0, tiled=True)

    squared = dot(warm_start, warm_start)
    fourth = dot(squared, squared)
    frobenius = jnp.sqrt(jnp.sum(statistic * statistic) + 1e-06)
    identity = jnp.eye(width, dtype=jnp.float32)
    scaled = statistic / frobenius + DAMPING * identity
    coupled = dot(fourth, scaled)
    factor = (5.0 * identity - coupled) * 0.25
    estimate = dot(warm_rows, factor)
    iterations = counts[2 * blocks[worker] + core]

    def second_step():
        factor_sq = dot(factor, factor)
        coupled_next = dot(factor_sq, dot(factor_sq, coupled))
        factor_next = (5.0 * identity - coupled_next) * 0.25
        return dot(estimate, factor_next)

    root_rows = lax.cond(iterations >= 2, second_step, lambda: estimate)
    root_sent = jnp.where(even, root_rows[half:], root_rows[:half])
    root_kept = jnp.where(even, root_rows[:half], root_rows[half:])
    root_got = lax.ppermute(root_sent, "core", SWAP)
    result = jnp.where(
        even, jnp.stack([root_kept, root_got]), jnp.stack([root_got, root_kept])
    )
    return result[None]


def solution(mesh):
    cores = 2
    x_count = 4
    dp_count, worker_count = mesh.devices.shape
    chips = Mesh(
        mesh.devices.reshape(dp_count // cores, cores, x_count, worker_count // x_count),
        ("y", "core", "x", "z"),
    )
    dp = ("y", "core")
    return jax.shard_map(
        local,
        mesh=chips,
        in_specs=(
            P(dp, WORKER, None, None),
            P(WORKER, None, dp, None),
            P(WORKER, None, dp, None),
            P(),
            P(),
            P(),
        ),
        out_specs=P(WORKER, None, dp, None),
        check_vma=False,
    )
```

```python
import jax
import jax.numpy as jnp
from jax import lax
from jax.experimental import pallas as pl
from jax.experimental.pallas import tpu as pltpu
from jax.sharding import Mesh, PartitionSpec as P

HISTORY = 0.5
DAMPING = 0.001
WORKER = ("x", "z")
PLANE = ("y", "x", "z")
SWAP = [(0, 1), (1, 0)]


def dot(first, second):
    return jnp.dot(
        first, second, precision=lax.Precision.HIGHEST, preferred_element_type=jnp.float32
    )


SMEM = pl.BlockSpec(memory_space=pltpu.SMEM)
VMEM = pl.BlockSpec(memory_space=pltpu.VMEM)


def to_tiles(rows):
    height, width = rows.shape
    tiles = rows.reshape(height // 8, 8, width // 128, 128).transpose(0, 2, 1, 3)
    return tiles.reshape(-1, 8, 128)


def from_tiles(tiles, width):
    split = tiles.reshape(-1, width // 128, 8, 128).transpose(0, 2, 1, 3)
    return split.reshape(-1, width)


def deliver_kernel(block_ref, piece_ref, out_ref):
    for reader in range(out_ref.shape[1]):
        block = block_ref[reader]
        total = piece_ref[0, block]
        for term in range(1, piece_ref.shape[0]):
            total = total + piece_ref[term, block]
        for copy in range(out_ref.shape[0]):
            out_ref[copy, reader] = total


def deliver(blocks, pieces):
    return pl.pallas_call(
        deliver_kernel,
        out_shape=jax.ShapeDtypeStruct(pieces.shape, pieces.dtype),
        in_specs=[SMEM, VMEM],
        out_specs=VMEM,
    )(blocks, pieces)


def warm_kernel(owner_ref, mine_ref, own_ref, sibling_ref, out_ref):
    for reader in range(out_ref.shape[0]):
        owner = owner_ref[reader]
        out_ref[reader] = jnp.where(mine_ref[reader] != 0, own_ref[owner], sibling_ref[owner])


def pick_warm(owners, mine, own_slot, sibling_slot):
    return pl.pallas_call(
        warm_kernel,
        out_shape=jax.ShapeDtypeStruct(own_slot.shape, own_slot.dtype),
        in_specs=[SMEM, SMEM, VMEM, VMEM],
        out_specs=VMEM,
    )(owners, mine, own_slot, sibling_slot)


def local(grad, prev_stats, warm_roots, owner_items, counts, read_shard):
    gradients = grad[:, 0]
    width = gradients.shape[-1]
    y_count = lax.axis_size("y")
    y = lax.axis_index("y")
    core = lax.axis_index("core")
    worker = lax.axis_index(WORKER)
    even = core == 0
    share = width // y_count
    half = share // 2
    weight = (1.0 - HISTORY) / (y_count * 2 * gradients.shape[0])

    left = jnp.einsum("mik,mjk->ij", gradients, gradients, preferred_element_type=jnp.float32)
    right = jnp.einsum("mki,mkj->ij", gradients, gradients, preferred_element_type=jnp.float32)
    place = (jnp.arange(width, dtype=jnp.int32) // half == y * 2 + core)[:, None]
    previous = HISTORY * prev_stats[0]

    def partial(first_kind):
        gram = weight * jnp.where(first_kind, left, right)
        rows = jnp.where(first_kind, previous[0], previous[1])
        rows = jnp.broadcast_to(rows[None], (width // half, half, width)).reshape(width, width)
        return gram + jnp.where(place, rows, 0.0)

    chip_sum = partial(even) + lax.ppermute(partial(~even), "core", SWAP)
    tiles = to_tiles(chip_sum)

    ids = jnp.arange(read_shard.shape[0], dtype=jnp.int32)
    blocks = jnp.sum(jnp.where(read_shard[None, :] == ids[:, None], ids[None, :], 0), 1)
    matches = owner_items[None] == (2 * blocks + core)[:, None, None]
    owners = jnp.sum(jnp.where(matches, ids[None, :, None], 0), (1, 2))
    slots = jnp.sum(jnp.where(matches, jnp.arange(2, dtype=jnp.int32), 0), (1, 2))
    mine = (slots == core).astype(jnp.int32)

    warm = warm_roots[0]
    warm_got = lax.ppermute(jnp.where(even, warm[1], warm[0]), "core", SWAP)
    warm_kept = jnp.where(even, warm[0], warm[1])
    own_warm = jnp.where(
        even,
        jnp.concatenate([warm_kept, warm_got], 0),
        jnp.concatenate([warm_got, warm_kept], 0),
    )
    own_slot = lax.all_to_all(to_tiles(own_warm), WORKER, 0, 0, tiled=True)
    sibling_slot = lax.ppermute(own_slot, "core", SWAP)
    warm_tiles = pick_warm(owners, mine, own_slot, sibling_slot)
    warm_rows = from_tiles(lax.all_to_all(warm_tiles, WORKER, 0, 0, tiled=True), width)
    warm_start = lax.all_gather(warm_rows, "y", axis=0, tiled=True)

    pieces = lax.all_to_all(tiles, PLANE, 0, 0, tiled=True).reshape((y_count, -1) + tiles.shape[1:])
    tiles = lax.all_to_all(
        deliver(blocks, pieces).reshape(tiles.shape), PLANE, 0, 0, tiled=True
    )
    statistic = from_tiles(tiles, width)

    squared = dot(warm_start, warm_start)
    fourth = dot(squared, squared)
    frobenius = jnp.sqrt(jnp.sum(statistic * statistic) + 1e-06)
    identity = jnp.eye(width, dtype=jnp.float32)
    scaled = statistic / frobenius + DAMPING * identity
    coupled = dot(fourth, scaled)
    factor = (5.0 * identity - coupled) * 0.25
    estimate = dot(warm_rows, factor)
    iterations = counts[2 * blocks[worker] + core]

    def second_step():
        factor_sq = dot(factor, factor)
        coupled_next = dot(factor_sq, dot(factor_sq, coupled))
        factor_next = (5.0 * identity - coupled_next) * 0.25
        return dot(estimate, factor_next)

    root_rows = lax.cond(iterations >= 2, second_step, lambda: estimate)
    root_sent = jnp.where(even, root_rows[half:], root_rows[:half])
    root_kept = jnp.where(even, root_rows[:half], root_rows[half:])
    root_got = lax.ppermute(root_sent, "core", SWAP)
    result = jnp.where(
        even, jnp.stack([root_kept, root_got]), jnp.stack([root_got, root_kept])
    )
    return result[None]


def solution(mesh):
    cores = 2
    x_count = 4
    dp_count, worker_count = mesh.devices.shape
    chips = Mesh(
        mesh.devices.reshape(dp_count // cores, cores, x_count, worker_count // x_count),
        ("y", "core", "x", "z"),
    )
    dp = ("y", "core")
    return jax.shard_map(
        local,
        mesh=chips,
        in_specs=(
            P(dp, WORKER, None, None),
            P(WORKER, None, dp, None),
            P(WORKER, None, dp, None),
            P(),
            P(),
            P(),
        ),
        out_specs=P(WORKER, None, dp, None),
        check_vma=False,
    )
```

```python
import jax
import jax.numpy as jnp
from jax import lax
from jax.experimental import pallas as pl
from jax.experimental.pallas import tpu as pltpu
from jax.sharding import Mesh, PartitionSpec as P

HISTORY = 0.5
DAMPING = 0.001
WORKER = ("x", "z")
PLANE = ("y", "x", "z")
SWAP = [(0, 1), (1, 0)]
BLOCK = 128
SMEM = pl.BlockSpec(memory_space=pltpu.SMEM)
VMEM = pl.BlockSpec(memory_space=pltpu.VMEM)


def dot(first, second, precision=lax.Precision.HIGHEST):
    return jnp.dot(first, second, precision=precision, preferred_element_type=jnp.float32)


def shape_of(*shape):
    return jax.ShapeDtypeStruct(shape, jnp.float32)


def upper_blocks(width):
    count = width // BLOCK
    pairs = [(i, j) for i in range(count) for j in range(i, count)]
    return [
        (pl.ds(number * BLOCK, BLOCK), pl.ds(i * BLOCK, BLOCK), pl.ds(j * BLOCK, BLOCK))
        for number, (i, j) in enumerate(pairs)
    ]


def upper_kernel(weight, core_ref, left_ref, right_ref, kept_ref, sent_ref):
    even = core_ref[0] == 0
    for packed, rows, columns in upper_blocks(left_ref.shape[0]):
        left = left_ref[rows, columns] * weight
        right = right_ref[rows, columns] * weight
        kept_ref[packed, :] = jnp.where(even, left, right)
        sent_ref[packed, :] = jnp.where(even, right, left)


def pack_upper(core, left, right, weight):
    rows = len(upper_blocks(left.shape[0])) * BLOCK

    def kernel(*refs):
        upper_kernel(weight, *refs)

    return pl.pallas_call(
        kernel,
        out_shape=[shape_of(rows, BLOCK)] * 2,
        in_specs=[SMEM, VMEM, VMEM],
        out_specs=[VMEM] * 2,
    )(core, left, right)


def scaled_kernel(packed_ref, carried_ref, out_ref):
    width = out_ref.shape[0]
    share = carried_ref.shape[2]

    def previous(rows, columns):
        first = rows.start // share
        parts = [carried_ref[first + n, 1, :, columns] for n in range(BLOCK // share)]
        return HISTORY * jnp.concatenate(parts, 0)

    total = jnp.zeros((1, BLOCK), jnp.float32)
    for packed, rows, columns in upper_blocks(width):
        sums = packed_ref[packed, :]
        value = sums + previous(rows, columns)
        out_ref[rows, columns] = value
        total = total + jnp.sum(value * value, axis=0, keepdims=True)
        if rows.start != columns.start:
            value = sums.T + previous(columns, rows)
            out_ref[columns, rows] = value
            total = total + jnp.sum(value * value, axis=0, keepdims=True)
    inverse = 1.0 / jnp.sqrt(jnp.sum(total, axis=1, keepdims=True) + 1e-06)
    row = lax.broadcasted_iota(jnp.int32, (BLOCK, width), 0)
    column = lax.broadcasted_iota(jnp.int32, (BLOCK, width), 1)
    for first in range(0, width, BLOCK):
        diagonal = jnp.where(column == row + first, DAMPING, 0.0)
        out_ref[pl.ds(first, BLOCK), :] = out_ref[pl.ds(first, BLOCK), :] * inverse + diagonal


def scaled_statistic(packed, carried):
    width = carried.shape[-1]
    return pl.pallas_call(
        scaled_kernel,
        out_shape=shape_of(width, width),
        in_specs=[VMEM] * 2,
        out_specs=VMEM,
    )(packed, carried)


def deliver_kernel(block_ref, piece_ref, out_ref):
    readers = block_ref.shape[0]
    copies = piece_ref.shape[0] // readers
    for reader in range(readers):
        block = block_ref[reader]
        total = piece_ref[block]
        for term in range(1, copies):
            total = total + piece_ref[term * readers + block]
        for copy in range(copies):
            out_ref[copy * readers + reader] = total


def deliver(blocks, pieces):
    return pl.pallas_call(
        deliver_kernel,
        out_shape=shape_of(*pieces.shape),
        in_specs=[SMEM, VMEM],
        out_specs=VMEM,
    )(blocks, pieces)


def spread_kernel(warm_ref, prev_ref, out_ref):
    for number, in_ref in enumerate((warm_ref, prev_ref)):
        _, rows, width = in_ref.shape
        for half in range(2):
            for j in range(out_ref.shape[0]):
                i, t = divmod(j, width // BLOCK)
                out_ref[j, number, pl.ds(4 * half, 4), :] = in_ref[
                    half, pl.ds(4 * i, 4), pl.ds(BLOCK * t, BLOCK)
                ]


def spread_tiles(warm, prev):
    count = warm.shape[1] * warm.shape[2] // (4 * BLOCK)
    return pl.pallas_call(
        spread_kernel,
        out_shape=shape_of(count, 2, 8, BLOCK),
        in_specs=[VMEM] * 2,
        out_specs=VMEM,
    )(warm, prev)


def pick_kernel(block_ref, owner_ref, slot_ref, tile_ref, out_ref):
    for reader in range(out_ref.shape[0]):
        for kind in range(2):
            place = 2 * reader + kind
            first = pl.multiple_of(4 * slot_ref[place], 4)
            out_ref[reader, 0, pl.ds(4 * kind, 4), :] = tile_ref[
                owner_ref[place], 0, pl.ds(first, 4), :
            ]
        out_ref[reader, 1] = tile_ref[block_ref[reader], 1]


def pick(blocks, owners, slots, tiles):
    return pl.pallas_call(
        pick_kernel,
        out_shape=shape_of(*tiles.shape),
        in_specs=[SMEM] * 3 + [VMEM],
        out_specs=VMEM,
    )(blocks, owners, slots, tiles)


def rows_kernel(core_ref, tile_ref, kept_ref, sent_ref):
    width = kept_ref.shape[2]
    for out_ref, kind in ((kept_ref, core_ref[0]), (sent_ref, 1 - core_ref[0])):
        first = pl.multiple_of(4 * kind, 4)
        for number in range(2):
            for j in range(tile_ref.shape[0]):
                i, t = divmod(j, width // BLOCK)
                out_ref[number, pl.ds(4 * i, 4), pl.ds(BLOCK * t, BLOCK)] = tile_ref[
                    j, number, pl.ds(first, 4), :
                ]


def rows_of_kinds(core, tiles, rows, width):
    return pl.pallas_call(
        rows_kernel,
        out_shape=[shape_of(2, rows, width)] * 2,
        in_specs=[SMEM, VMEM],
        out_specs=[VMEM] * 2,
    )(core, tiles)


def local(grad, prev_stats, warm_roots, owner_items, counts, read_shard):
    gradients = grad[:, 0]
    width = gradients.shape[-1]
    y_count = lax.axis_size("y")
    core = lax.axis_index("core")
    worker = lax.axis_index(WORKER)
    even = core == 0
    core_place = core.reshape(1)
    share = width // y_count
    half = share // 2
    weight = (1.0 - HISTORY) / (y_count * 2 * gradients.shape[0])

    ids = jnp.arange(read_shard.shape[0], dtype=jnp.int32)
    blocks = jnp.sum(jnp.where(read_shard[None, :] == ids[:, None], ids[None, :], 0), 1)
    items = (2 * blocks[:, None] + jnp.arange(2, dtype=jnp.int32)).reshape(-1)
    matches = owner_items[None] == items[:, None, None]
    owners = jnp.sum(jnp.where(matches, ids[None, :, None], 0), (1, 2))
    slots = jnp.sum(jnp.where(matches, jnp.arange(2, dtype=jnp.int32), 0), (1, 2))

    tiles = spread_tiles(warm_roots[0], prev_stats[0])
    tiles = lax.all_to_all(tiles, WORKER, 0, 0, tiled=True)
    tiles = lax.all_to_all(pick(blocks, owners, slots, tiles), WORKER, 0, 0, tiled=True)
    kept, sent = rows_of_kinds(core_place, tiles, half, width)
    got = lax.ppermute(sent, "core", SWAP)
    carried = jnp.where(
        even, jnp.concatenate([kept, got], 1), jnp.concatenate([got, kept], 1)
    )
    warm_rows = carried[0]
    carried = lax.all_gather(carried, "y", axis=0, tiled=False)
    warm_start = carried[:, 0].reshape(width, width)

    left = jnp.einsum("mik,mjk->ij", gradients, gradients, preferred_element_type=jnp.float32)
    right = jnp.einsum("mki,mkj->ij", gradients, gradients, preferred_element_type=jnp.float32)
    kept, sent = pack_upper(core_place, left, right, weight)
    packed = kept + lax.ppermute(sent, "core", SWAP)
    peers = y_count * read_shard.shape[0]
    pieces = lax.all_to_all(packed.reshape(peers, 1, -1), PLANE, 0, 0, tiled=True)
    pieces = lax.all_to_all(deliver(blocks, pieces), PLANE, 0, 0, tiled=True)
    scaled = scaled_statistic(pieces.reshape(packed.shape), carried)

    squared = dot(warm_start, warm_start)
    fourth = dot(squared, squared)
    identity = jnp.eye(width, dtype=jnp.float32)
    coupled = dot(fourth, scaled)
    factor = (5.0 * identity - coupled) * 0.25
    high = lax.Precision.HIGH
    estimate = dot(warm_rows, factor, high)
    iterations = counts[2 * blocks[worker] + core]

    def second_step():
        factor_sq = dot(factor, factor, high)
        coupled_next = dot(factor_sq, dot(factor_sq, coupled, high), high)
        factor_next = (5.0 * identity - coupled_next) * 0.25
        return dot(estimate, factor_next, high)

    root_rows = lax.cond(iterations >= 2, second_step, lambda: estimate)
    root_sent = jnp.where(even, root_rows[half:], root_rows[:half])
    root_kept = jnp.where(even, root_rows[:half], root_rows[half:])
    root_got = lax.ppermute(root_sent, "core", SWAP)
    result = jnp.where(
        even, jnp.stack([root_kept, root_got]), jnp.stack([root_got, root_kept])
    )
    return result[None]


def solution(mesh):
    cores = 2
    x_count = 4
    dp_count, worker_count = mesh.devices.shape
    chips = Mesh(
        mesh.devices.reshape(dp_count // cores, cores, x_count, worker_count // x_count),
        ("y", "core", "x", "z"),
    )
    dp = ("y", "core")
    return jax.shard_map(
        local,
        mesh=chips,
        in_specs=(
            P(dp, WORKER, None, None),
            P(WORKER, None, dp, None),
            P(WORKER, None, dp, None),
            P(),
            P(),
            P(),
        ),
        out_specs=P(WORKER, None, dp, None),
        check_vma=False,
    )
```

```python
import jax
import jax.numpy as jnp
from jax import lax
from jax.experimental import pallas as pl
from jax.experimental.pallas import tpu as pltpu
from jax.sharding import Mesh, PartitionSpec as P

HISTORY = 0.5
DAMPING = 0.001
WORKER = ("x", "z")
PLANE = ("y", "x", "z")
SWAP = [(0, 1), (1, 0)]
LANES = 128
HALF_LANES = 64
TILE = 8
SMEM = pl.BlockSpec(memory_space=pltpu.SMEM)
VMEM = pl.BlockSpec(memory_space=pltpu.VMEM)


def dot(first, second, precision=lax.Precision.HIGHEST):
    return jnp.dot(first, second, precision=precision, preferred_element_type=jnp.float32)


def shape_of(*shape):
    return jax.ShapeDtypeStruct(shape, jnp.float32)


def low_lanes(rows=TILE):
    return lax.broadcasted_iota(jnp.int32, (rows, LANES), 1) < HALF_LANES


def turn(value):
    return pltpu.roll(value, HALF_LANES, 1)


def tile_columns(width):
    return [pl.ds(LANES * t, LANES) for t in range(width // LANES)]


def pair_kinds(low, first, second):
    return (
        jnp.where(low, first, turn(second)),
        jnp.where(low, turn(first), second),
    )


def halves_kernel(weight, place_ref, left_ref, right_ref, prev_ref, kept_ref, sent_ref):
    y, core = place_ref[0], place_ref[1]
    half = prev_ref.shape[1]
    columns = tile_columns(left_ref.shape[1])
    messages = 2 * len(columns)
    groups = half // TILE
    low = low_lanes()
    for chunk in range(left_ref.shape[0] // (2 * half)):
        for out_ref, part in ((kept_ref, core), (sent_ref, 1 - core)):
            for group in range(groups):
                first = pl.multiple_of(2 * half * chunk + half * part + TILE * group, TILE)
                for t, lanes in enumerate(columns):
                    left = left_ref[pl.ds(first, TILE), lanes] * weight
                    right = right_ref[pl.ds(first, TILE), lanes] * weight
                    number = (chunk * groups + group) * messages + 2 * t
                    out_ref[number], out_ref[number + 1] = pair_kinds(low, left, right)
    for group in range(groups):
        rows = pl.ds(TILE * group, TILE)
        for t, lanes in enumerate(columns):
            pair = pair_kinds(
                low, HISTORY * prev_ref[0, rows, lanes], HISTORY * prev_ref[1, rows, lanes]
            )
            number = (y * groups + group) * messages + 2 * t
            kept_ref[number] += pair[0]
            kept_ref[number + 1] += pair[1]


def split_halves(place, left, right, prev, weight):
    messages = left.shape[0] * left.shape[1] // (TILE * LANES)

    def kernel(*refs):
        halves_kernel(weight, *refs)

    return pl.pallas_call(
        kernel,
        out_shape=[shape_of(messages, TILE, LANES)] * 2,
        in_specs=[SMEM, VMEM, VMEM, VMEM],
        out_specs=[VMEM] * 2,
    )(place, left, right, prev)


def message_kernel(place_ref, kept_ref, got_ref, warm_ref, out_ref):
    y = place_ref[0]
    columns = tile_columns(warm_ref.shape[2])
    workers = kept_ref.shape[0] // TILE
    for number in range(kept_ref.shape[0]):
        chunk, worker = divmod(number, workers)
        first = (TILE + 1) * number
        out_ref[pl.ds(first, TILE), :] = kept_ref[number] + got_ref[number]
        slot = (y + chunk) % 2
        row = (chunk // 2) * (workers // len(columns)) + worker // len(columns)
        out_ref[pl.ds(first + TILE, 1), :] = warm_ref[
            slot, pl.ds(row, 1), columns[worker % len(columns)]
        ]


def build_messages(place, kept, got, warm):
    return pl.pallas_call(
        message_kernel,
        out_shape=shape_of(kept.shape[0] * (TILE + 1), LANES),
        in_specs=[SMEM, VMEM, VMEM, VMEM],
        out_specs=VMEM,
    )(place, kept, got, warm)


def deliver_kernel(place_ref, block_ref, owner_ref, slot_ref, in_ref, out_ref, sum_ref, row_ref):
    y = place_ref[0]
    workers = block_ref.shape[0]
    chunks = in_ref.shape[0] // (workers * (TILE + 1))
    stride = workers * (TILE + 1)
    low = low_lanes()
    upper = lax.broadcasted_iota(jnp.int32, (TILE, LANES), 0) < TILE // 2
    for worker in range(workers):
        first = (TILE + 1) * worker
        total = in_ref[pl.ds(first, TILE), :]
        for chunk in range(1, chunks):
            total = total + in_ref[pl.ds(first + stride * chunk, TILE), :]
        sum_ref[worker] = total
    for number in range(chunks * workers):
        row_ref[number] = in_ref[pl.ds((TILE + 1) * number + TILE, 1), :]
    for reader in range(workers):
        tile = sum_ref[block_ref[reader]]
        for kind in range(2):
            place = 2 * reader + kind
            parity = (slot_ref[place] + y) % 2
            rows = [
                row_ref[(2 * n + parity) * workers + owner_ref[place]]
                for n in range(chunks // 2)
            ]
            warm = jnp.concatenate(rows + rows, 0)
            warm = jnp.where(upper, turn(warm), warm)
            value = jnp.where(low, tile if kind == 0 else turn(tile), warm)
            for chunk in range(kind, chunks, 2):
                out_ref[chunk * workers + reader] = value


def deliver(place, blocks, owners, slots, messages):
    workers = blocks.shape[0]
    count = messages.shape[0] // (TILE + 1)
    return pl.pallas_call(
        deliver_kernel,
        out_shape=shape_of(count, TILE, LANES),
        in_specs=[SMEM] * 4 + [VMEM],
        out_specs=VMEM,
        scratch_shapes=[
            pltpu.VMEM((workers, TILE, LANES), jnp.float32),
            pltpu.VMEM((count, 1, LANES), jnp.float32),
        ],
    )(place, blocks, owners, slots, messages)


def whole_kernel(place_ref, own_ref, other_ref, scaled_ref, warm_ref):
    core, slot = place_ref[1], place_ref[2]
    width = scaled_ref.shape[0]
    columns = tile_columns(width)
    count = len(columns)
    chunks = TILE
    workers = own_ref.shape[0] // TILE // chunks
    share = width // chunks
    half = share // 2
    groups = half // TILE
    low = low_lanes()
    total = jnp.zeros((TILE, LANES), jnp.float32)
    for part in range(2):
        own = core == part

        def read(rows):
            return jnp.where(own, own_ref[rows, :], other_ref[rows, :])

        for chunk in range(chunks):
            for group in range(groups):
                for t, lanes in enumerate(columns):
                    number = chunk * workers + (group * count + t) * 2
                    value = jnp.where(
                        low,
                        read(pl.ds(TILE * number, TILE)),
                        turn(read(pl.ds(TILE * (number + 1), TILE))),
                    )
                    first = share * chunk + half * part + TILE * group
                    scaled_ref[pl.ds(first, TILE), lanes] = value
                    total = total + value * value
            parity = (slot + chunk) % 2
            for t, lanes in enumerate(columns):
                for n in range(chunks // 2):
                    start = TILE * (chunk * workers + t) + n
                    lower = read(pl.ds(start, TILE, stride=TILE * count))
                    higher = read(pl.ds(start + TILE // 2, TILE, stride=TILE * count))
                    first = share * (2 * n + parity) + half * part + TILE * (chunk // 2)
                    first = pl.multiple_of(first, TILE)
                    warm_ref[pl.ds(first, TILE), lanes] = jnp.where(low, turn(lower), higher)
    total = jnp.sum(jnp.sum(total, axis=0, keepdims=True), axis=1, keepdims=True)
    inverse = 1.0 / jnp.sqrt(total + 1e-06)
    row = lax.broadcasted_iota(jnp.int32, (share, width), 0)
    column = lax.broadcasted_iota(jnp.int32, (share, width), 1)
    for first in range(0, width, share):
        diagonal = jnp.where(column == row + first, DAMPING, 0.0)
        scaled_ref[pl.ds(first, share), :] = scaled_ref[pl.ds(first, share), :] * inverse + diagonal


def whole(place, own, other, width):
    return pl.pallas_call(
        whole_kernel,
        out_shape=[shape_of(width, width)] * 2,
        in_specs=[SMEM, VMEM, VMEM],
        out_specs=[VMEM] * 2,
    )(place, own, other)


def local(grad, prev_stats, warm_roots, owner_items, counts, read_shard):
    gradients = grad[:, 0]
    width = gradients.shape[-1]
    y_count = lax.axis_size("y")
    y = lax.axis_index("y")
    core = lax.axis_index("core")
    worker = lax.axis_index(WORKER)
    half = width // y_count // 2
    kind = y % 2
    weight = (1.0 - HISTORY) / (y_count * 2 * gradients.shape[0])

    ids = jnp.arange(read_shard.shape[0], dtype=jnp.int32)
    blocks = jnp.sum(jnp.where(read_shard[None, :] == ids[:, None], ids[None, :], 0), 1)
    items = (2 * blocks[:, None] + jnp.arange(2, dtype=jnp.int32)).reshape(-1)
    matches = owner_items[None] == items[:, None, None]
    owners = jnp.sum(jnp.where(matches, ids[None, :, None], 0), (1, 2))
    slots = jnp.sum(jnp.where(matches, jnp.arange(2, dtype=jnp.int32), 0), (1, 2))
    place = jnp.stack([y, core, slots[2 * worker + kind]])
    iterations = counts[2 * blocks[worker] + kind]

    left = jnp.einsum("mik,mjk->ij", gradients, gradients, preferred_element_type=jnp.float32)
    right = jnp.einsum("mki,mkj->ij", gradients, gradients, preferred_element_type=jnp.float32)
    kept, sent = split_halves(place, left, right, prev_stats[0], weight)
    got = lax.ppermute(sent, "core", SWAP)
    messages = build_messages(place, kept, got, warm_roots[0])
    peers = kept.shape[0]
    arrived = lax.all_to_all(messages.reshape(peers, 1, -1), PLANE, 0, 0, tiled=True)

    tiles = deliver(place, blocks, owners, slots, arrived.reshape(messages.shape))
    own = lax.all_to_all(tiles, PLANE, 0, 0, tiled=True)
    other = lax.ppermute(own, "core", SWAP)
    scaled, warm_start = whole(
        place, own.reshape(-1, LANES), other.reshape(-1, LANES), width
    )

    squared = dot(warm_start, warm_start)
    fourth = dot(squared, squared)
    identity = jnp.eye(width, dtype=jnp.float32)
    coupled = dot(fourth, scaled)
    factor = (5.0 * identity - coupled) * 0.25
    high = lax.Precision.HIGH
    warm_rows = lax.dynamic_slice(
        warm_start.reshape(y_count, 2, half, width), (y - kind, core, 0, 0), (2, 1, half, width)
    )
    estimate = dot(warm_rows.reshape(2 * half, width), factor, high)

    def second_step():
        factor_sq = dot(factor, factor, high)
        coupled_next = dot(factor_sq, dot(factor_sq, coupled, high), high)
        factor_next = (5.0 * identity - coupled_next) * 0.25
        return dot(estimate, factor_next, high)

    root_rows = lax.cond(iterations >= 2, second_step, lambda: estimate)
    first = kind == 0
    root_sent = jnp.where(first, root_rows[half:], root_rows[:half])
    root_kept = jnp.where(first, root_rows[:half], root_rows[half:])
    root_got = lax.ppermute(root_sent, "y", [(i, i ^ 1) for i in range(y_count)])
    result = jnp.where(
        first, jnp.stack([root_kept, root_got]), jnp.stack([root_got, root_kept])
    )
    return result[None]


def solution(mesh):
    cores = 2
    x_count = 4
    dp_count, worker_count = mesh.devices.shape
    chips = Mesh(
        mesh.devices.reshape(dp_count // cores, cores, x_count, worker_count // x_count),
        ("y", "core", "x", "z"),
    )
    dp = ("y", "core")
    return jax.shard_map(
        local,
        mesh=chips,
        in_specs=(
            P(dp, WORKER, None, None),
            P(WORKER, None, dp, None),
            P(WORKER, None, dp, None),
            P(),
            P(),
            P(),
        ),
        out_specs=P(WORKER, None, dp, None),
        check_vma=False,
    )
```

```python
import jax
import jax.numpy as jnp
from jax import lax
from jax.experimental import pallas as pl
from jax.experimental.pallas import tpu as pltpu
from jax.sharding import Mesh, PartitionSpec as P

HISTORY = 0.5
DAMPING = 0.001
WORKER = ("x", "z")
PLANE = ("yh", "yl", "x", "z")
LINE = ("yl", "x", "z")
SWAP = [(0, 1), (1, 0)]
LANES = 128
TILE = 8
EXTRA = 2
SMEM = pl.BlockSpec(memory_space=pltpu.SMEM)
VMEM = pl.BlockSpec(memory_space=pltpu.VMEM)
PARAMS = pltpu.CompilerParams(vmem_limit_bytes=12 * 1024 * 1024)


def dot(first, second, precision=lax.Precision.HIGHEST):
    return jnp.dot(first, second, precision=precision, preferred_element_type=jnp.float32)


def shape_of(*shape):
    return jax.ShapeDtypeStruct(shape, jnp.float32)


def tile_columns(width):
    return [pl.ds(LANES * t, LANES) for t in range(width // LANES)]


def halves_kernel(weight, place_ref, left_ref, right_ref, prev_ref, kept_ref, sent_ref):
    y, core = place_ref[0], place_ref[1]
    width = left_ref.shape[1]
    half = prev_ref.shape[1]
    groups = half // TILE
    columns = tile_columns(width)
    chunks = left_ref.shape[0] // (2 * half)
    count = chunks * groups * len(columns)
    for out_ref, part in ((kept_ref, core), (sent_ref, 1 - core)):
        for chunk in range(chunks):
            for group in range(groups):
                first = pl.multiple_of(2 * half * chunk + half * part + TILE * group, TILE)
                for t, lanes in enumerate(columns):
                    number = (chunk * groups + group) * len(columns) + t
                    out_ref[number] = left_ref[pl.ds(first, TILE), lanes] * weight
                    out_ref[count + number] = right_ref[pl.ds(first, TILE), lanes] * weight
    for kind in range(2):
        for group in range(groups):
            for t, lanes in enumerate(columns):
                number = (y * groups + group) * len(columns) + t + count * kind
                kept_ref[number] += HISTORY * prev_ref[kind, pl.ds(TILE * group, TILE), lanes]


def split_halves(place, left, right, prev, weight):
    messages = left.shape[0] * left.shape[1] // (TILE * LANES)

    def kernel(*refs):
        halves_kernel(weight, *refs)

    return pl.pallas_call(
        kernel,
        out_shape=[shape_of(messages, TILE, LANES)] * 2,
        in_specs=[SMEM, VMEM, VMEM, VMEM],
        out_specs=[VMEM] * 2,
        compiler_params=PARAMS,
    )(place, left, right, prev)


def message_kernel(kept_ref, got_ref, warm_ref, out_ref):
    _, rows, width = warm_ref.shape
    columns = tile_columns(width)
    size = TILE + EXTRA
    for number in range(kept_ref.shape[0]):
        out_ref[pl.ds(size * number, TILE), :] = kept_ref[number] + got_ref[number]
    for kind in range(2):
        for slot in range(EXTRA):
            for t, lanes in enumerate(columns):
                for first in range(0, rows, TILE):
                    number = (kind * rows + first) * len(columns) + t
                    out_ref[
                        pl.ds(size * number + TILE + slot, TILE, stride=size * len(columns)), :
                    ] = warm_ref[slot, pl.ds(first, TILE), lanes]


def build_messages(kept, got, warm):
    return pl.pallas_call(
        message_kernel,
        out_shape=shape_of(kept.shape[0] * (TILE + EXTRA), LANES),
        in_specs=[VMEM] * 3,
        out_specs=VMEM,
        compiler_params=PARAMS,
    )(kept, got, warm)


def deliver_kernel(kind_ref, block_ref, owner_ref, slot_ref, in_ref, out_ref, dense_ref, sum_ref, warm_ref):
    kind = kind_ref[0]
    workers = block_ref.shape[0]
    size = TILE + EXTRA
    stride = workers * size
    chunks = in_ref.shape[0] // stride
    for first in range(0, stride, TILE):
        total = in_ref[pl.ds(first, TILE), :]
        for chunk in range(1, chunks):
            total = total + in_ref[pl.ds(first + stride * chunk, TILE), :]
        dense_ref[pl.ds(first, TILE), :] = total
    for worker in range(workers):
        sum_ref[worker] = dense_ref[pl.ds(size * worker, TILE), :]
        for slot in range(EXTRA):
            first = size * worker + TILE + slot
            warm_ref[EXTRA * worker + slot] = in_ref[pl.ds(first, chunks, stride=stride), :]
    for reader in range(workers):
        place = 2 * reader + kind
        sums = sum_ref[block_ref[reader]]
        warm = warm_ref[EXTRA * owner_ref[place] + slot_ref[place]]
        for number in range(reader, out_ref.shape[0], workers):
            out_ref[number, pl.ds(0, TILE), :] = sums
            out_ref[number, pl.ds(TILE, TILE), :] = warm


def deliver(kind, blocks, owners, slots, messages):
    workers = blocks.shape[0]
    rows = messages.shape[0]
    return pl.pallas_call(
        deliver_kernel,
        out_shape=shape_of(rows // (TILE + EXTRA) // 2, 2 * TILE, LANES),
        in_specs=[SMEM] * 4 + [VMEM],
        out_specs=VMEM,
        scratch_shapes=[
            pltpu.VMEM((workers * (TILE + EXTRA), LANES), jnp.float32),
            pltpu.VMEM((workers, TILE, LANES), jnp.float32),
            pltpu.VMEM((workers * EXTRA, TILE, LANES), jnp.float32),
        ],
        compiler_params=PARAMS,
    )(kind, blocks, owners, slots, messages)


def whole_kernel(core_ref, own_ref, other_ref, scaled_ref, warm_ref):
    width = scaled_ref.shape[0]
    columns = tile_columns(width)
    chunks = TILE
    share = width // chunks
    half = share // 2
    groups = half // TILE

    def assemble(*halves):
        total = jnp.zeros((TILE, LANES), jnp.float32)
        for part, in_ref in enumerate(halves):
            for chunk in range(chunks):
                for group in range(groups):
                    rows = pl.ds(share * chunk + half * part + TILE * group, TILE)
                    for t, lanes in enumerate(columns):
                        number = (chunk * groups + group) * len(columns) + t
                        value = in_ref[pl.ds(2 * TILE * number, TILE), :]
                        scaled_ref[rows, lanes] = value
                        total = total + value * value
                        first = 2 * TILE * (TILE * group * len(columns) + t) + TILE + chunk
                        warm_ref[rows, lanes] = in_ref[
                            pl.ds(first, TILE, stride=2 * TILE * len(columns)), :
                        ]
        total = jnp.sum(jnp.sum(total, axis=0, keepdims=True), axis=1, keepdims=True)
        inverse = 1.0 / jnp.sqrt(total + 1e-06)
        row = lax.broadcasted_iota(jnp.int32, (share, width), 0)
        column = lax.broadcasted_iota(jnp.int32, (share, width), 1)
        for first in range(0, width, share):
            diagonal = jnp.where(column == row + first, DAMPING, 0.0)
            rows = pl.ds(first, share)
            scaled_ref[rows, :] = scaled_ref[rows, :] * inverse + diagonal

    @pl.when(core_ref[0] == 0)
    def _():
        assemble(own_ref, other_ref)

    @pl.when(core_ref[0] != 0)
    def _():
        assemble(other_ref, own_ref)


def whole(core, own, other, width):
    return pl.pallas_call(
        whole_kernel,
        out_shape=[shape_of(width, width)] * 2,
        in_specs=[SMEM, VMEM, VMEM],
        out_specs=[VMEM] * 2,
        compiler_params=PARAMS,
    )(core, own, other)


def local(grad, prev_stats, warm_roots, owner_items, counts, read_shard):
    gradients = grad[:, 0]
    width = gradients.shape[-1]
    kinds, lines = lax.axis_size("yh"), lax.axis_size("yl")
    y_count = kinds * lines
    kind = lax.axis_index("yh")
    y = kind * lines + lax.axis_index("yl")
    core = lax.axis_index("core")
    worker = lax.axis_index(WORKER)
    half = width // y_count // 2
    weight = (1.0 - HISTORY) / (y_count * 2 * gradients.shape[0])

    left = jnp.einsum("mik,mjk->ij", gradients, gradients, preferred_element_type=jnp.float32)
    right = jnp.einsum("mki,mkj->ij", gradients, gradients, preferred_element_type=jnp.float32)
    kept, sent = split_halves(jnp.stack([y, core]), left, right, prev_stats[0], weight)
    got = lax.ppermute(sent, "core", SWAP)
    messages = build_messages(kept, got, warm_roots[0])
    peers = kept.shape[0]
    arrived = lax.all_to_all(messages.reshape(peers, 1, -1), PLANE, 0, 0, tiled=True)

    ids = jnp.arange(read_shard.shape[0], dtype=jnp.int32)
    blocks = jnp.sum(jnp.where(read_shard[None, :] == ids[:, None], ids[None, :], 0), 1)
    items = (2 * blocks[:, None] + jnp.arange(2, dtype=jnp.int32)).reshape(-1)
    matches = owner_items[None] == items[:, None, None]
    owners = jnp.sum(jnp.where(matches, ids[None, :, None], 0), (1, 2))
    slots = jnp.sum(jnp.where(matches, jnp.arange(2, dtype=jnp.int32), 0), (1, 2))
    iterations = counts[2 * blocks[worker] + kind]

    tiles = deliver(
        kind.reshape(1), blocks, owners, slots, arrived.reshape(messages.shape)
    )
    own = lax.all_to_all(tiles, LINE, 0, 0, tiled=True)
    other = lax.ppermute(own, "core", SWAP)
    scaled, warm_start = whole(
        core.reshape(1), own.reshape(-1, LANES), other.reshape(-1, LANES), width
    )

    squared = dot(warm_start, warm_start)
    fourth = dot(squared, squared)
    identity = jnp.eye(width, dtype=jnp.float32)
    coupled = dot(fourth, scaled)
    factor = (5.0 * identity - coupled) * 0.25
    high = lax.Precision.HIGH
    warm_rows = lax.dynamic_slice(
        warm_start.reshape(kinds, lines, 2, half, width),
        (0, y - kind * lines, core, 0, 0),
        (kinds, 1, 1, half, width),
    )
    estimate = dot(warm_rows.reshape(kinds * half, width), factor, high)

    def second_step():
        factor_sq = dot(factor, factor, high)
        coupled_next = dot(factor_sq, dot(factor_sq, coupled, high), high)
        factor_next = (5.0 * identity - coupled_next) * 0.25
        return dot(estimate, factor_next, high)

    root_rows = lax.cond(iterations >= 2, second_step, lambda: estimate)
    first = kind == 0
    root_sent = jnp.where(first, root_rows[half:], root_rows[:half])
    root_kept = jnp.where(first, root_rows[:half], root_rows[half:])
    root_got = lax.ppermute(root_sent, "yh", SWAP)
    result = jnp.where(
        first, jnp.stack([root_kept, root_got]), jnp.stack([root_got, root_kept])
    )
    return result[None]


def solution(mesh):
    kinds, cores, x_count = 2, 2, 4
    dp_count, worker_count = mesh.devices.shape
    chips = Mesh(
        mesh.devices.reshape(
            kinds, dp_count // (kinds * cores), cores, x_count, worker_count // x_count
        ),
        ("yh", "yl", "core", "x", "z"),
    )
    dp = ("yh", "yl", "core")
    return jax.shard_map(
        local,
        mesh=chips,
        in_specs=(
            P(dp, WORKER, None, None),
            P(WORKER, None, dp, None),
            P(WORKER, None, dp, None),
            P(),
            P(),
            P(),
        ),
        out_specs=P(WORKER, None, dp, None),
        check_vma=False,
    )
```

```python
import jax
import jax.numpy as jnp
from jax import lax
from jax.experimental import pallas as pl
from jax.experimental.pallas import tpu as pltpu
from jax.sharding import Mesh, PartitionSpec as P

HISTORY = 0.5
DAMPING = 0.001
WORKER = ("x", "z")
PLANE = ("x", "z", "yh", "yl")
LINE = ("x", "z", "yl")
SWAP = [(0, 1), (1, 0)]
LANES = 128
TILE = 8
EXTRA = 2
SMEM = pl.BlockSpec(memory_space=pltpu.SMEM)
VMEM = pl.BlockSpec(memory_space=pltpu.VMEM)
PARAMS = pltpu.CompilerParams(vmem_limit_bytes=5 * 1024 * 1024)


def dot(first, second, precision=lax.Precision.HIGHEST):
    return jnp.dot(first, second, precision=precision, preferred_element_type=jnp.float32)


def shape_of(*shape):
    return jax.ShapeDtypeStruct(shape, jnp.float32)


def tile_columns(width):
    return [pl.ds(LANES * t, LANES) for t in range(width // LANES)]


def halves_kernel(weight, place_ref, left_ref, right_ref, prev_ref, kept_ref, sent_ref):
    y, core = place_ref[0], place_ref[1]
    width = left_ref.shape[1]
    half = prev_ref.shape[1]
    groups = half // TILE
    columns = tile_columns(width)
    chunks = left_ref.shape[0] // (2 * half)
    count = chunks * groups * len(columns)
    for out_ref, part in ((kept_ref, core), (sent_ref, 1 - core)):
        for chunk in range(chunks):
            for group in range(groups):
                first = pl.multiple_of(2 * half * chunk + half * part + TILE * group, TILE)
                for t, lanes in enumerate(columns):
                    number = (chunk * groups + group) * len(columns) + t
                    out_ref[number] = left_ref[pl.ds(first, TILE), lanes] * weight
                    out_ref[count + number] = right_ref[pl.ds(first, TILE), lanes] * weight
    for kind in range(2):
        for group in range(groups):
            for t, lanes in enumerate(columns):
                number = (y * groups + group) * len(columns) + t + count * kind
                kept_ref[number] += HISTORY * prev_ref[kind, pl.ds(TILE * group, TILE), lanes]


def split_halves(place, left, right, prev, weight):
    messages = left.shape[0] * left.shape[1] // (TILE * LANES)

    def kernel(*refs):
        halves_kernel(weight, *refs)

    return pl.pallas_call(
        kernel,
        out_shape=[shape_of(messages, TILE, LANES)] * 2,
        in_specs=[SMEM, VMEM, VMEM, VMEM],
        out_specs=[VMEM] * 2,
        compiler_params=PARAMS,
    )(place, left, right, prev)


def message_kernel(kept_ref, got_ref, warm_ref, out_ref):
    columns = tile_columns(warm_ref.shape[2])
    size = TILE + EXTRA
    chunks = TILE
    workers = kept_ref.shape[0] // chunks
    for number in range(kept_ref.shape[0]):
        chunk, worker = divmod(number, workers)
        first = size * (chunks * worker + chunk)
        out_ref[pl.ds(first, TILE), :] = kept_ref[number] + got_ref[number]
    for chunk in range(chunks):
        rows = pl.ds(TILE * (chunk % (chunks // 2)), TILE)
        for slot in range(EXTRA):
            for t, lanes in enumerate(columns):
                first = size * (chunks * t + chunk) + TILE + slot
                out_ref[
                    pl.ds(first, TILE, stride=size * chunks * len(columns)), :
                ] = warm_ref[slot, rows, lanes]


def build_messages(kept, got, warm):
    return pl.pallas_call(
        message_kernel,
        out_shape=shape_of(kept.shape[0] * (TILE + EXTRA), LANES),
        in_specs=[VMEM] * 3,
        out_specs=VMEM,
        compiler_params=PARAMS,
    )(kept, got, warm)


def deliver_kernel(kind_ref, block_ref, owner_ref, slot_ref, in_ref, out_ref, sum_ref, warm_ref):
    kind = kind_ref[0]
    workers = block_ref.shape[0]
    size = TILE + EXTRA
    chunks = in_ref.shape[0] // (workers * size)
    copies = out_ref.shape[0] // workers
    for worker in range(workers):
        base = size * chunks * worker
        total = in_ref[pl.ds(base, TILE), :]
        for chunk in range(1, chunks):
            total = total + in_ref[pl.ds(base + size * chunk, TILE), :]
        sum_ref[worker] = total
        for slot in range(EXTRA):
            first = base + TILE + slot
            warm_ref[EXTRA * worker + slot] = in_ref[pl.ds(first, chunks, stride=size), :]
    for reader in range(workers):
        place = 2 * reader + kind
        sums = sum_ref[block_ref[reader]]
        warm = warm_ref[EXTRA * owner_ref[place] + slot_ref[place]]
        for number in range(copies * reader, copies * (reader + 1)):
            out_ref[number, pl.ds(0, TILE), :] = sums
            out_ref[number, pl.ds(TILE, TILE), :] = warm


def deliver(kind, blocks, owners, slots, messages):
    workers = blocks.shape[0]
    rows = messages.shape[0]
    return pl.pallas_call(
        deliver_kernel,
        out_shape=shape_of(rows // (TILE + EXTRA) // 2, 2 * TILE, LANES),
        in_specs=[SMEM] * 4 + [VMEM],
        out_specs=VMEM,
        scratch_shapes=[
            pltpu.VMEM((workers, TILE, LANES), jnp.float32),
            pltpu.VMEM((workers * EXTRA, TILE, LANES), jnp.float32),
        ],
        compiler_params=PARAMS,
    )(kind, blocks, owners, slots, messages)


def whole_kernel(core_ref, own_ref, other_ref, scaled_ref, warm_ref):
    width = scaled_ref.shape[0]
    columns = tile_columns(width)
    chunks = TILE
    share = width // chunks
    half = share // 2
    groups = half // TILE

    def assemble(*halves):
        total = jnp.zeros((TILE, LANES), jnp.float32)
        size = 2 * TILE
        lines = chunks // 2
        for part, in_ref in enumerate(halves):
            for chunk in range(chunks):
                for group in range(groups):
                    rows = pl.ds(share * chunk + half * part + TILE * group, TILE)
                    for t, lanes in enumerate(columns):
                        line, worker = divmod(
                            (chunk * groups + group) * len(columns) + t, TILE * len(columns)
                        )
                        value = in_ref[pl.ds(size * (lines * worker + line), TILE), :]
                        scaled_ref[rows, lanes] = value
                        total = total + value * value
                        first = size * (lines * t + group) + TILE + chunk
                        warm_ref[rows, lanes] = in_ref[
                            pl.ds(first, TILE, stride=size * lines * len(columns)), :
                        ]
        total = jnp.sum(jnp.sum(total, axis=0, keepdims=True), axis=1, keepdims=True)
        inverse = 1.0 / jnp.sqrt(total + 1e-06)
        row = lax.broadcasted_iota(jnp.int32, (share, width), 0)
        column = lax.broadcasted_iota(jnp.int32, (share, width), 1)
        for first in range(0, width, share):
            diagonal = jnp.where(column == row + first, DAMPING, 0.0)
            rows = pl.ds(first, share)
            scaled_ref[rows, :] = scaled_ref[rows, :] * inverse + diagonal

    @pl.when(core_ref[0] == 0)
    def _():
        assemble(own_ref, other_ref)

    @pl.when(core_ref[0] != 0)
    def _():
        assemble(other_ref, own_ref)


def whole(core, own, other, width):
    return pl.pallas_call(
        whole_kernel,
        out_shape=[shape_of(width, width)] * 2,
        in_specs=[SMEM, VMEM, VMEM],
        out_specs=[VMEM] * 2,
        compiler_params=PARAMS,
    )(core, own, other)


def local(grad, prev_stats, warm_roots, owner_items, counts, read_shard):
    gradients = grad[:, 0]
    width = gradients.shape[-1]
    kinds, lines = lax.axis_size("yh"), lax.axis_size("yl")
    y_count = kinds * lines
    kind = lax.axis_index("yh")
    y = kind * lines + lax.axis_index("yl")
    core = lax.axis_index("core")
    worker = lax.axis_index(WORKER)
    half = width // y_count // 2
    weight = (1.0 - HISTORY) / (y_count * 2 * gradients.shape[0])

    left = jnp.einsum("mik,mjk->ij", gradients, gradients, preferred_element_type=jnp.float32)
    right = jnp.einsum("mki,mkj->ij", gradients, gradients, preferred_element_type=jnp.float32)
    kept, sent = split_halves(jnp.stack([y, core]), left, right, prev_stats[0], weight)
    got = lax.ppermute(sent, "core", SWAP)
    messages = build_messages(kept, got, warm_roots[0])
    peers = kept.shape[0]
    arrived = lax.all_to_all(messages.reshape(peers, 1, -1), PLANE, 0, 0, tiled=True)

    ids = jnp.arange(read_shard.shape[0], dtype=jnp.int32)
    blocks = jnp.sum(jnp.where(read_shard[None, :] == ids[:, None], ids[None, :], 0), 1)
    items = (2 * blocks[:, None] + jnp.arange(2, dtype=jnp.int32)).reshape(-1)
    matches = owner_items[None] == items[:, None, None]
    owners = jnp.sum(jnp.where(matches, ids[None, :, None], 0), (1, 2))
    slots = jnp.sum(jnp.where(matches, jnp.arange(2, dtype=jnp.int32), 0), (1, 2))
    iterations = counts[2 * blocks[worker] + kind]

    tiles = deliver(
        kind.reshape(1), blocks, owners, slots, arrived.reshape(messages.shape)
    )
    own = lax.all_to_all(tiles, LINE, 0, 0, tiled=True)
    other = lax.ppermute(own, "core", SWAP)
    scaled, warm_start = whole(
        core.reshape(1), own.reshape(-1, LANES), other.reshape(-1, LANES), width
    )

    squared = dot(warm_start, warm_start)
    fourth = dot(squared, squared)
    identity = jnp.eye(width, dtype=jnp.float32)
    coupled = dot(fourth, scaled)
    factor = (5.0 * identity - coupled) * 0.25
    high = lax.Precision.HIGH
    warm_rows = lax.dynamic_slice(
        warm_start.reshape(kinds, lines, 2, half, width),
        (0, y - kind * lines, core, 0, 0),
        (kinds, 1, 1, half, width),
    )
    estimate = dot(warm_rows.reshape(kinds * half, width), factor, high)

    def second_step():
        rows = estimate
        for matrix in (factor, factor, factor, factor, coupled):
            rows = dot(rows, matrix, high)
        return (5.0 * estimate - rows) * 0.25

    root_rows = lax.cond(iterations >= 2, second_step, lambda: estimate)
    first = kind == 0
    root_sent = jnp.where(first, root_rows[half:], root_rows[:half])
    root_kept = jnp.where(first, root_rows[:half], root_rows[half:])
    root_got = lax.ppermute(root_sent, "yh", SWAP)
    result = jnp.where(
        first, jnp.stack([root_kept, root_got]), jnp.stack([root_got, root_kept])
    )
    return result[None]


def solution(mesh):
    kinds, cores, x_count = 2, 2, 4
    dp_count, worker_count = mesh.devices.shape
    chips = Mesh(
        mesh.devices.reshape(
            kinds, dp_count // (kinds * cores), cores, x_count, worker_count // x_count
        ),
        ("yh", "yl", "core", "x", "z"),
    )
    dp = ("yh", "yl", "core")
    return jax.shard_map(
        local,
        mesh=chips,
        in_specs=(
            P(dp, WORKER, None, None),
            P(WORKER, None, dp, None),
            P(WORKER, None, dp, None),
            P(),
            P(),
            P(),
        ),
        out_specs=P(WORKER, None, dp, None),
        check_vma=False,
    )
```

```python
import jax
import jax.numpy as jnp
from jax import lax
from jax.experimental import pallas as pl
from jax.experimental.pallas import tpu as pltpu
from jax.sharding import Mesh, PartitionSpec as P

HISTORY = 0.5
DAMPING = 0.001
WORKER = ("x", "z")
PLANE = ("yh", "yl", "x", "z")
LINE = ("yl", "x", "z")
SWAP = [(0, 1), (1, 0)]
LANES = 128
TILE = 8
EXTRA = 2
SMEM = pl.BlockSpec(memory_space=pltpu.SMEM)
VMEM = pl.BlockSpec(memory_space=pltpu.VMEM)
PARAMS = pltpu.CompilerParams(vmem_limit_bytes=8 * 1024 * 1024)


def dot(first, second, precision=lax.Precision.HIGHEST):
    return jnp.dot(first, second, precision=precision, preferred_element_type=jnp.float32)


def shape_of(*shape):
    return jax.ShapeDtypeStruct(shape, jnp.float32)


def tile_columns(width):
    return [pl.ds(LANES * t, LANES) for t in range(width // LANES)]


def halves_kernel(weight, place_ref, grad_ref, prev_ref, kept_ref, sent_ref, gram_ref):
    y, core = place_ref[0], place_ref[1]
    terms, width, _ = grad_ref.shape
    half = prev_ref.shape[1]
    groups = half // TILE
    columns = tile_columns(width)
    chunks = width // (2 * half)
    count = chunks * groups * len(columns)
    step = 2 * LANES
    for kind in range(2):
        for first in range(0, width, step):
            part = pl.ds(first, step)
            total = jnp.zeros((step, width), jnp.float32)
            for term in range(terms):
                if kind == 0:
                    rows, axis = grad_ref[term, part, :], 1
                else:
                    rows, axis = grad_ref[term, :, part], 0
                total = total + lax.dot_general(
                    rows,
                    grad_ref[term],
                    (((axis,), (axis,)), ((), ())),
                    preferred_element_type=jnp.float32,
                )
            gram_ref[kind, part, :] = total * weight
    for out_ref, part in ((kept_ref, core), (sent_ref, 1 - core)):
        for kind in range(2):
            for chunk in range(chunks):
                for group in range(groups):
                    first = pl.multiple_of(2 * half * chunk + half * part + TILE * group, TILE)
                    for t, lanes in enumerate(columns):
                        number = (chunk * groups + group) * len(columns) + t + count * kind
                        out_ref[number] = gram_ref[kind, pl.ds(first, TILE), lanes]
    for kind in range(2):
        for group in range(groups):
            for t, lanes in enumerate(columns):
                number = (y * groups + group) * len(columns) + t + count * kind
                kept_ref[number] += HISTORY * prev_ref[kind, pl.ds(TILE * group, TILE), lanes]


def gram_halves(place, gradients, prev, weight):
    width = gradients.shape[1]
    messages = width * width // (TILE * LANES)

    def kernel(*refs):
        halves_kernel(weight, *refs)

    return pl.pallas_call(
        kernel,
        out_shape=[shape_of(messages, TILE, LANES)] * 2,
        in_specs=[SMEM, VMEM, VMEM],
        out_specs=[VMEM] * 2,
        scratch_shapes=[pltpu.VMEM((2, width, width), jnp.float32)],
        compiler_params=PARAMS,
    )(place, gradients, prev)


def message_kernel(kept_ref, got_ref, warm_ref, out_ref):
    _, rows, width = warm_ref.shape
    columns = tile_columns(width)
    size = TILE + EXTRA
    for number in range(kept_ref.shape[0]):
        out_ref[pl.ds(size * number, TILE), :] = kept_ref[number] + got_ref[number]
    for kind in range(2):
        for slot in range(EXTRA):
            for t, lanes in enumerate(columns):
                for first in range(0, rows, TILE):
                    number = (kind * rows + first) * len(columns) + t
                    out_ref[
                        pl.ds(size * number + TILE + slot, TILE, stride=size * len(columns)), :
                    ] = warm_ref[slot, pl.ds(first, TILE), lanes]


def build_messages(kept, got, warm):
    return pl.pallas_call(
        message_kernel,
        out_shape=shape_of(kept.shape[0] * (TILE + EXTRA), LANES),
        in_specs=[VMEM] * 3,
        out_specs=VMEM,
        compiler_params=PARAMS,
    )(kept, got, warm)


def deliver_kernel(kind_ref, block_ref, owner_ref, slot_ref, in_ref, out_ref, dense_ref, sum_ref, warm_ref):
    kind = kind_ref[0]
    workers = block_ref.shape[0]
    size = TILE + EXTRA
    stride = workers * size
    chunks = in_ref.shape[0] // stride
    for first in range(0, stride, TILE):
        total = in_ref[pl.ds(first, TILE), :]
        for chunk in range(1, chunks):
            total = total + in_ref[pl.ds(first + stride * chunk, TILE), :]
        dense_ref[pl.ds(first, TILE), :] = total
    for worker in range(workers):
        sum_ref[worker] = dense_ref[pl.ds(size * worker, TILE), :]
        for slot in range(EXTRA):
            first = size * worker + TILE + slot
            warm_ref[EXTRA * worker + slot] = in_ref[pl.ds(first, chunks, stride=stride), :]
    for reader in range(workers):
        place = 2 * reader + kind
        sums = sum_ref[block_ref[reader]]
        warm = warm_ref[EXTRA * owner_ref[place] + slot_ref[place]]
        for number in range(reader, out_ref.shape[0], workers):
            out_ref[number, pl.ds(0, TILE), :] = sums
            out_ref[number, pl.ds(TILE, TILE), :] = warm


def deliver(kind, blocks, owners, slots, messages):
    workers = blocks.shape[0]
    rows = messages.shape[0]
    return pl.pallas_call(
        deliver_kernel,
        out_shape=shape_of(rows // (TILE + EXTRA) // 2, 2 * TILE, LANES),
        in_specs=[SMEM] * 4 + [VMEM],
        out_specs=VMEM,
        scratch_shapes=[
            pltpu.VMEM((workers * (TILE + EXTRA), LANES), jnp.float32),
            pltpu.VMEM((workers, TILE, LANES), jnp.float32),
            pltpu.VMEM((workers * EXTRA, TILE, LANES), jnp.float32),
        ],
        compiler_params=PARAMS,
    )(kind, blocks, owners, slots, messages)


def whole_kernel(core_ref, own_ref, other_ref, scaled_ref, warm_ref):
    width = scaled_ref.shape[0]
    columns = tile_columns(width)
    chunks = TILE
    share = width // chunks
    half = share // 2
    groups = half // TILE

    def assemble(*halves):
        total = jnp.zeros((TILE, LANES), jnp.float32)
        for part, in_ref in enumerate(halves):
            for chunk in range(chunks):
                for group in range(groups):
                    rows = pl.ds(share * chunk + half * part + TILE * group, TILE)
                    for t, lanes in enumerate(columns):
                        number = (chunk * groups + group) * len(columns) + t
                        value = in_ref[pl.ds(2 * TILE * number, TILE), :]
                        scaled_ref[rows, lanes] = value
                        total = total + value * value
                        first = 2 * TILE * (TILE * group * len(columns) + t) + TILE + chunk
                        warm_ref[rows, lanes] = in_ref[
                            pl.ds(first, TILE, stride=2 * TILE * len(columns)), :
                        ]
        total = jnp.sum(jnp.sum(total, axis=0, keepdims=True), axis=1, keepdims=True)
        inverse = 1.0 / jnp.sqrt(total + 1e-06)
        row = lax.broadcasted_iota(jnp.int32, (share, width), 0)
        column = lax.broadcasted_iota(jnp.int32, (share, width), 1)
        for first in range(0, width, share):
            diagonal = jnp.where(column == row + first, DAMPING, 0.0)
            rows = pl.ds(first, share)
            scaled_ref[rows, :] = scaled_ref[rows, :] * inverse + diagonal

    @pl.when(core_ref[0] == 0)
    def _():
        assemble(own_ref, other_ref)

    @pl.when(core_ref[0] != 0)
    def _():
        assemble(other_ref, own_ref)


def whole(core, own, other, width):
    return pl.pallas_call(
        whole_kernel,
        out_shape=[shape_of(width, width)] * 2,
        in_specs=[SMEM, VMEM, VMEM],
        out_specs=[VMEM] * 2,
        compiler_params=PARAMS,
    )(core, own, other)


def local(grad, prev_stats, warm_roots, owner_items, counts, read_shard):
    gradients = grad[:, 0]
    width = gradients.shape[-1]
    kinds, lines = lax.axis_size("yh"), lax.axis_size("yl")
    y_count = kinds * lines
    kind = lax.axis_index("yh")
    y = kind * lines + lax.axis_index("yl")
    core = lax.axis_index("core")
    worker = lax.axis_index(WORKER)
    half = width // y_count // 2
    weight = (1.0 - HISTORY) / (y_count * 2 * gradients.shape[0])

    kept, sent = gram_halves(jnp.stack([y, core]), gradients, prev_stats[0], weight)
    got = lax.ppermute(sent, "core", SWAP)
    messages = build_messages(kept, got, warm_roots[0])
    peers = kept.shape[0]
    arrived = lax.all_to_all(messages.reshape(peers, 1, -1), PLANE, 0, 0, tiled=True)

    ids = jnp.arange(read_shard.shape[0], dtype=jnp.int32)
    blocks = jnp.sum(jnp.where(read_shard[None, :] == ids[:, None], ids[None, :], 0), 1)
    items = (2 * blocks[:, None] + jnp.arange(2, dtype=jnp.int32)).reshape(-1)
    matches = owner_items[None] == items[:, None, None]
    owners = jnp.sum(jnp.where(matches, ids[None, :, None], 0), (1, 2))
    slots = jnp.sum(jnp.where(matches, jnp.arange(2, dtype=jnp.int32), 0), (1, 2))
    iterations = counts[2 * blocks[worker] + kind]

    tiles = deliver(
        kind.reshape(1), blocks, owners, slots, arrived.reshape(messages.shape)
    )
    own = lax.all_to_all(tiles, LINE, 0, 0, tiled=True)
    other = lax.ppermute(own, "core", SWAP)
    scaled, warm_start = whole(
        core.reshape(1), own.reshape(-1, LANES), other.reshape(-1, LANES), width
    )

    squared = dot(warm_start, warm_start)
    fourth = dot(squared, squared)
    identity = jnp.eye(width, dtype=jnp.float32)
    coupled = dot(fourth, scaled)
    factor = (5.0 * identity - coupled) * 0.25
    high = lax.Precision.HIGH
    warm_rows = lax.dynamic_slice(
        warm_start.reshape(kinds, lines, 2, half, width),
        (0, y - kind * lines, core, 0, 0),
        (kinds, 1, 1, half, width),
    )
    estimate = dot(warm_rows.reshape(kinds * half, width), factor, high)

    def second_step():
        rows = estimate
        for matrix in (factor, factor, factor, factor, coupled):
            rows = dot(rows, matrix, high)
        return (5.0 * estimate - rows) * 0.25

    root_rows = lax.cond(iterations >= 2, second_step, lambda: estimate)
    first = kind == 0
    root_sent = jnp.where(first, root_rows[half:], root_rows[:half])
    root_kept = jnp.where(first, root_rows[:half], root_rows[half:])
    root_got = lax.ppermute(root_sent, "yh", SWAP)
    result = jnp.where(
        first, jnp.stack([root_kept, root_got]), jnp.stack([root_got, root_kept])
    )
    return result[None]


def solution(mesh):
    kinds, cores, x_count = 2, 2, 4
    dp_count, worker_count = mesh.devices.shape
    chips = Mesh(
        mesh.devices.reshape(
            kinds, dp_count // (kinds * cores), cores, x_count, worker_count // x_count
        ),
        ("yh", "yl", "core", "x", "z"),
    )
    dp = ("yh", "yl", "core")
    return jax.shard_map(
        local,
        mesh=chips,
        in_specs=(
            P(dp, WORKER, None, None),
            P(WORKER, None, dp, None),
            P(WORKER, None, dp, None),
            P(),
            P(),
            P(),
        ),
        out_specs=P(WORKER, None, dp, None),
        check_vma=False,
    )
```

```python
import jax
import jax.numpy as jnp
from jax import lax
from jax.experimental import pallas as pl
from jax.experimental.pallas import tpu as pltpu
from jax.sharding import Mesh, PartitionSpec as P

HISTORY = 0.5
DAMPING = 0.001
WORKER = ("x", "z")
PLANE = ("yh", "yl", "x", "z")
LINE = ("yl", "x", "z")
SWAP = [(0, 1), (1, 0)]
LANES = 128
TILE = 8
EXTRA = 2
SMEM = pl.BlockSpec(memory_space=pltpu.SMEM)
VMEM = pl.BlockSpec(memory_space=pltpu.VMEM)
PARAMS = pltpu.CompilerParams(vmem_limit_bytes=8 * 1024 * 1024)


def dot(first, second, precision=lax.Precision.HIGHEST):
    return jnp.dot(first, second, precision=precision, preferred_element_type=jnp.float32)


def shape_of(*shape):
    return jax.ShapeDtypeStruct(shape, jnp.float32)


def tile_columns(width):
    return [pl.ds(LANES * t, LANES) for t in range(width // LANES)]


def halves_kernel(weight, half, core_ref, grad_ref, kept_ref, sent_ref, gram_ref):
    core = core_ref[0]
    terms, width, _ = grad_ref.shape
    groups = half // TILE
    columns = tile_columns(width)
    chunks = width // (2 * half)
    count = chunks * groups * len(columns)
    step = 2 * LANES
    for kind in range(2):
        for first in range(0, width, step):
            part = pl.ds(first, step)
            total = jnp.zeros((step, width), jnp.float32)
            for term in range(terms):
                if kind == 0:
                    rows, axis = grad_ref[term, part, :], 1
                else:
                    rows, axis = grad_ref[term, :, part], 0
                total = total + lax.dot_general(
                    rows,
                    grad_ref[term],
                    (((axis,), (axis,)), ((), ())),
                    preferred_element_type=jnp.float32,
                )
            gram_ref[kind, part, :] = total * weight
    for out_ref, part in ((kept_ref, core), (sent_ref, 1 - core)):
        for kind in range(2):
            for chunk in range(chunks):
                for group in range(groups):
                    first = pl.multiple_of(2 * half * chunk + half * part + TILE * group, TILE)
                    for t, lanes in enumerate(columns):
                        number = (chunk * groups + group) * len(columns) + t + count * kind
                        out_ref[number] = gram_ref[kind, pl.ds(first, TILE), lanes]


def gram_halves(core, gradients, half, weight):
    width = gradients.shape[1]
    messages = width * width // (TILE * LANES)

    def kernel(*refs):
        halves_kernel(weight, half, *refs)

    return pl.pallas_call(
        kernel,
        out_shape=[shape_of(messages, TILE, LANES)] * 2,
        in_specs=[SMEM, VMEM],
        out_specs=[VMEM] * 2,
        scratch_shapes=[pltpu.VMEM((2, width, width), jnp.float32)],
        compiler_params=PARAMS,
    )(core, gradients)


def message_kernel(y_ref, kept_ref, got_ref, prev_ref, warm_ref, out_ref):
    _, rows, width = warm_ref.shape
    columns = tile_columns(width)
    size = TILE + EXTRA
    for number in range(kept_ref.shape[0]):
        out_ref[pl.ds(size * number, TILE), :] = kept_ref[number] + got_ref[number]
    count = kept_ref.shape[0] // 2
    shares = rows // TILE * len(columns)
    for kind in range(2):
        for part in range(shares):
            group, t = divmod(part, len(columns))
            number = count * kind + y_ref[0] * shares + part
            value = HISTORY * prev_ref[kind, pl.ds(TILE * group, TILE), columns[t]]
            out_ref[pl.ds(size * number, TILE), :] = kept_ref[number] + got_ref[number] + value
    for kind in range(2):
        for slot in range(EXTRA):
            for t, lanes in enumerate(columns):
                for first in range(0, rows, TILE):
                    number = (kind * rows + first) * len(columns) + t
                    out_ref[
                        pl.ds(size * number + TILE + slot, TILE, stride=size * len(columns)), :
                    ] = warm_ref[slot, pl.ds(first, TILE), lanes]


def build_messages(y, kept, got, prev, warm):
    return pl.pallas_call(
        message_kernel,
        out_shape=shape_of(kept.shape[0] * (TILE + EXTRA), LANES),
        in_specs=[SMEM] + [VMEM] * 4,
        out_specs=VMEM,
        compiler_params=PARAMS,
    )(y, kept, got, prev, warm)


def deliver_kernel(kind_ref, block_ref, owner_ref, slot_ref, in_ref, out_ref, dense_ref, sum_ref, warm_ref):
    kind = kind_ref[0]
    workers = block_ref.shape[0]
    size = TILE + EXTRA
    stride = workers * size
    chunks = in_ref.shape[0] // stride
    for first in range(0, stride, TILE):
        total = in_ref[pl.ds(first, TILE), :]
        for chunk in range(1, chunks):
            total = total + in_ref[pl.ds(first + stride * chunk, TILE), :]
        dense_ref[pl.ds(first, TILE), :] = total
    for worker in range(workers):
        sum_ref[worker] = dense_ref[pl.ds(size * worker, TILE), :]
        for slot in range(EXTRA):
            first = size * worker + TILE + slot
            warm_ref[EXTRA * worker + slot] = in_ref[pl.ds(first, chunks, stride=stride), :]
    for reader in range(workers):
        place = 2 * reader + kind
        sums = sum_ref[block_ref[reader]]
        warm = warm_ref[EXTRA * owner_ref[place] + slot_ref[place]]
        for number in range(reader, out_ref.shape[0], workers):
            out_ref[number, pl.ds(0, TILE), :] = sums
            out_ref[number, pl.ds(TILE, TILE), :] = warm


def deliver(kind, blocks, owners, slots, messages):
    workers = blocks.shape[0]
    rows = messages.shape[0]
    return pl.pallas_call(
        deliver_kernel,
        out_shape=shape_of(rows // (TILE + EXTRA) // 2, 2 * TILE, LANES),
        in_specs=[SMEM] * 4 + [VMEM],
        out_specs=VMEM,
        scratch_shapes=[
            pltpu.VMEM((workers * (TILE + EXTRA), LANES), jnp.float32),
            pltpu.VMEM((workers, TILE, LANES), jnp.float32),
            pltpu.VMEM((workers * EXTRA, TILE, LANES), jnp.float32),
        ],
        compiler_params=PARAMS,
    )(kind, blocks, owners, slots, messages)


def whole_kernel(core_ref, own_ref, other_ref, scaled_ref, warm_ref):
    width = scaled_ref.shape[0]
    columns = tile_columns(width)
    chunks = TILE
    share = width // chunks
    half = share // 2
    groups = half // TILE

    def assemble(*halves):
        total = jnp.zeros((TILE, LANES), jnp.float32)
        for part, in_ref in enumerate(halves):
            for chunk in range(chunks):
                for group in range(groups):
                    rows = pl.ds(share * chunk + half * part + TILE * group, TILE)
                    for t, lanes in enumerate(columns):
                        number = (chunk * groups + group) * len(columns) + t
                        value = in_ref[pl.ds(2 * TILE * number, TILE), :]
                        scaled_ref[rows, lanes] = value
                        total = total + value * value
                        first = 2 * TILE * (TILE * group * len(columns) + t) + TILE + chunk
                        warm_ref[rows, lanes] = in_ref[
                            pl.ds(first, TILE, stride=2 * TILE * len(columns)), :
                        ]
        total = jnp.sum(jnp.sum(total, axis=0, keepdims=True), axis=1, keepdims=True)
        inverse = 1.0 / jnp.sqrt(total + 1e-06)
        row = lax.broadcasted_iota(jnp.int32, (share, width), 0)
        column = lax.broadcasted_iota(jnp.int32, (share, width), 1)
        for first in range(0, width, share):
            diagonal = jnp.where(column == row + first, DAMPING, 0.0)
            rows = pl.ds(first, share)
            scaled_ref[rows, :] = scaled_ref[rows, :] * inverse + diagonal

    @pl.when(core_ref[0] == 0)
    def _():
        assemble(own_ref, other_ref)

    @pl.when(core_ref[0] != 0)
    def _():
        assemble(other_ref, own_ref)


def whole(core, own, other, width):
    return pl.pallas_call(
        whole_kernel,
        out_shape=[shape_of(width, width)] * 2,
        in_specs=[SMEM, VMEM, VMEM],
        out_specs=[VMEM] * 2,
        compiler_params=PARAMS,
    )(core, own, other)


def local(grad, prev_stats, warm_roots, owner_items, counts, read_shard):
    gradients = grad[:, 0]
    width = gradients.shape[-1]
    kinds, lines = lax.axis_size("yh"), lax.axis_size("yl")
    y_count = kinds * lines
    kind = lax.axis_index("yh")
    y = kind * lines + lax.axis_index("yl")
    core = lax.axis_index("core")
    worker = lax.axis_index(WORKER)
    half = width // y_count // 2
    weight = (1.0 - HISTORY) / (y_count * 2 * gradients.shape[0])

    kept, sent = gram_halves(core.reshape(1), gradients, half, weight)
    got = lax.ppermute(sent, "core", SWAP)
    messages = build_messages(y.reshape(1), kept, got, prev_stats[0], warm_roots[0])
    peers = kept.shape[0]
    arrived = lax.all_to_all(messages.reshape(peers, 1, -1), PLANE, 0, 0, tiled=True)

    ids = jnp.arange(read_shard.shape[0], dtype=jnp.int32)
    blocks = jnp.sum(jnp.where(read_shard[None, :] == ids[:, None], ids[None, :], 0), 1)
    items = (2 * blocks[:, None] + jnp.arange(2, dtype=jnp.int32)).reshape(-1)
    matches = owner_items[None] == items[:, None, None]
    owners = jnp.sum(jnp.where(matches, ids[None, :, None], 0), (1, 2))
    slots = jnp.sum(jnp.where(matches, jnp.arange(2, dtype=jnp.int32), 0), (1, 2))
    iterations = counts[2 * blocks[worker] + kind]

    tiles = deliver(
        kind.reshape(1), blocks, owners, slots, arrived.reshape(messages.shape)
    )
    own = lax.all_to_all(tiles, LINE, 0, 0, tiled=True)
    other = lax.ppermute(own, "core", SWAP)
    scaled, warm_start = whole(
        core.reshape(1), own.reshape(-1, LANES), other.reshape(-1, LANES), width
    )

    squared = dot(warm_start, warm_start)
    fourth = dot(squared, squared)
    identity = jnp.eye(width, dtype=jnp.float32)
    coupled = dot(fourth, scaled)
    factor = (5.0 * identity - coupled) * 0.25
    high = lax.Precision.HIGH
    across = y_count - 1 - y
    warm_rows = warm_start.reshape(y_count, 2, half, width)
    warm_rows = [
        lax.dynamic_slice(warm_rows, (chunk, core, 0, 0), (1, 1, half, width))
        for chunk in (y, across)
    ]
    warm_rows = jnp.concatenate(warm_rows, 0).reshape(2 * half, width)
    estimate = dot(warm_rows, factor, high)

    def second_step():
        rows = estimate
        for matrix in (factor, factor, factor, factor, coupled):
            rows = dot(rows, matrix, high)
        return (5.0 * estimate - rows) * 0.25

    root_rows = lax.cond(iterations >= 2, second_step, lambda: estimate)
    pairs = [(i, y_count - 1 - i) for i in range(y_count)]
    root_kept = root_rows[:half]
    root_got = lax.ppermute(root_rows[half:], ("yh", "yl"), pairs)
    result = jnp.where(
        kind == 0, jnp.stack([root_kept, root_got]), jnp.stack([root_got, root_kept])
    )
    return result[None]


def solution(mesh):
    kinds, cores, x_count = 2, 2, 4
    dp_count, worker_count = mesh.devices.shape
    chips = Mesh(
        mesh.devices.reshape(
            kinds, dp_count // (kinds * cores), cores, x_count, worker_count // x_count
        ),
        ("yh", "yl", "core", "x", "z"),
    )
    dp = ("yh", "yl", "core")
    return jax.shard_map(
        local,
        mesh=chips,
        in_specs=(
            P(dp, WORKER, None, None),
            P(WORKER, None, dp, None),
            P(WORKER, None, dp, None),
            P(),
            P(),
            P(),
        ),
        out_specs=P(WORKER, None, dp, None),
        check_vma=False,
    )
```

```python
import jax
import jax.numpy as jnp
from jax import lax
from jax.experimental import pallas as pl
from jax.experimental.pallas import tpu as pltpu
from jax.sharding import Mesh, PartitionSpec as P

HISTORY = 0.5
DAMPING = 0.001
WORKER = ("x", "z")
PLANE = ("yh", "yl", "x", "z")
LINE = ("yl", "x", "z")
SWAP = [(0, 1), (1, 0)]
LANES = 128
TILE = 8
EXTRA = 2
SMEM = pl.BlockSpec(memory_space=pltpu.SMEM)
VMEM = pl.BlockSpec(memory_space=pltpu.VMEM)
PARAMS = pltpu.CompilerParams(vmem_limit_bytes=8 * 1024 * 1024)


def shape_of(*shape):
    return jax.ShapeDtypeStruct(shape, jnp.float32)


def tile_columns(width):
    return [pl.ds(LANES * t, LANES) for t in range(width // LANES)]


def halves_kernel(weight, half, core_ref, grad_ref, kept_ref, sent_ref, gram_ref):
    core = core_ref[0]
    terms, width, _ = grad_ref.shape
    groups = half // TILE
    columns = tile_columns(width)
    chunks = width // (2 * half)
    count = chunks * groups * len(columns)
    step = 2 * LANES
    for kind in range(2):
        for first in range(0, width, step):
            part = pl.ds(first, step)
            total = jnp.zeros((step, width), jnp.float32)
            for term in range(terms):
                if kind == 0:
                    rows, axis = grad_ref[term, part, :], 1
                else:
                    rows, axis = grad_ref[term, :, part], 0
                total = total + lax.dot_general(
                    rows,
                    grad_ref[term],
                    (((axis,), (axis,)), ((), ())),
                    preferred_element_type=jnp.float32,
                )
            gram_ref[kind, part, :] = total * weight
    for out_ref, part in ((kept_ref, core), (sent_ref, 1 - core)):
        for kind in range(2):
            for chunk in range(chunks):
                for group in range(groups):
                    first = pl.multiple_of(2 * half * chunk + half * part + TILE * group, TILE)
                    for t, lanes in enumerate(columns):
                        number = (chunk * groups + group) * len(columns) + t + count * kind
                        out_ref[number] = gram_ref[kind, pl.ds(first, TILE), lanes]


def gram_halves(core, gradients, half, weight):
    width = gradients.shape[1]
    messages = width * width // (TILE * LANES)

    def kernel(*refs):
        halves_kernel(weight, half, *refs)

    return pl.pallas_call(
        kernel,
        out_shape=[shape_of(messages, TILE, LANES)] * 2,
        in_specs=[SMEM, VMEM],
        out_specs=[VMEM] * 2,
        scratch_shapes=[pltpu.VMEM((2, width, width), jnp.float32)],
        compiler_params=PARAMS,
    )(core, gradients)


def message_kernel(y_ref, kept_ref, got_ref, prev_ref, warm_ref, out_ref):
    _, rows, width = warm_ref.shape
    columns = tile_columns(width)
    size = TILE + EXTRA
    for number in range(kept_ref.shape[0]):
        out_ref[pl.ds(size * number, TILE), :] = kept_ref[number] + got_ref[number]
    count = kept_ref.shape[0] // 2
    shares = rows // TILE * len(columns)
    for kind in range(2):
        for part in range(shares):
            group, t = divmod(part, len(columns))
            number = count * kind + y_ref[0] * shares + part
            value = HISTORY * prev_ref[kind, pl.ds(TILE * group, TILE), columns[t]]
            out_ref[pl.ds(size * number, TILE), :] = kept_ref[number] + got_ref[number] + value
    for kind in range(2):
        for slot in range(EXTRA):
            for t, lanes in enumerate(columns):
                for first in range(0, rows, TILE):
                    number = (kind * rows + first) * len(columns) + t
                    out_ref[
                        pl.ds(size * number + TILE + slot, TILE, stride=size * len(columns)), :
                    ] = warm_ref[slot, pl.ds(first, TILE), lanes]


def build_messages(y, kept, got, prev, warm):
    return pl.pallas_call(
        message_kernel,
        out_shape=shape_of(kept.shape[0] * (TILE + EXTRA), LANES),
        in_specs=[SMEM] + [VMEM] * 4,
        out_specs=VMEM,
        compiler_params=PARAMS,
    )(y, kept, got, prev, warm)


def deliver_kernel(kind_ref, block_ref, owner_ref, slot_ref, in_ref, out_ref, dense_ref, sum_ref, warm_ref):
    kind = kind_ref[0]
    workers = block_ref.shape[0]
    size = TILE + EXTRA
    stride = workers * size
    chunks = in_ref.shape[0] // stride
    for first in range(0, stride, TILE):
        total = in_ref[pl.ds(first, TILE), :]
        for chunk in range(1, chunks):
            total = total + in_ref[pl.ds(first + stride * chunk, TILE), :]
        dense_ref[pl.ds(first, TILE), :] = total
    for worker in range(workers):
        sum_ref[worker] = dense_ref[pl.ds(size * worker, TILE), :]
        for slot in range(EXTRA):
            first = size * worker + TILE + slot
            warm_ref[EXTRA * worker + slot] = in_ref[pl.ds(first, chunks, stride=stride), :]
    for reader in range(workers):
        place = 2 * reader + kind
        sums = sum_ref[block_ref[reader]]
        warm = warm_ref[EXTRA * owner_ref[place] + slot_ref[place]]
        for number in range(reader, out_ref.shape[0], workers):
            out_ref[number, pl.ds(0, TILE), :] = sums
            out_ref[number, pl.ds(TILE, TILE), :] = warm


def deliver(kind, blocks, owners, slots, messages):
    workers = blocks.shape[0]
    rows = messages.shape[0]
    return pl.pallas_call(
        deliver_kernel,
        out_shape=shape_of(rows // (TILE + EXTRA) // 2, 2 * TILE, LANES),
        in_specs=[SMEM] * 4 + [VMEM],
        out_specs=VMEM,
        scratch_shapes=[
            pltpu.VMEM((workers * (TILE + EXTRA), LANES), jnp.float32),
            pltpu.VMEM((workers, TILE, LANES), jnp.float32),
            pltpu.VMEM((workers * EXTRA, TILE, LANES), jnp.float32),
        ],
        compiler_params=PARAMS,
    )(kind, blocks, owners, slots, messages)


def cut(value, parts):
    pieces = []
    for number in range(parts):
        piece = value.astype(jnp.bfloat16)
        pieces.append(piece)
        if number < parts - 1:
            value = value - piece.astype(jnp.float32)
    return pieces


def cut_into(out_ref, parts, value_of):
    width = out_ref.shape[1]
    for first in range(0, width, LANES):
        for number, piece in enumerate(cut(value_of(first), parts)):
            out_ref[number, pl.ds(first, LANES), :] = piece


def product(left, right, parts):
    total = None
    for order in reversed(range(parts)):
        for number in range(order + 1):
            term = jnp.dot(
                left[number], right(order - number), preferred_element_type=jnp.float32
            )
            total = term if total is None else total + term
    return total


def newton_kernel(
    core_ref, y_ref, count_ref, own_ref, other_ref, out_ref, scaled_ref, work_ref, left_ref, right_ref
):
    width = scaled_ref.shape[0]
    columns = tile_columns(width)
    chunks = TILE
    share = width // chunks
    half = share // 2
    groups = half // TILE
    step = 2 * LANES

    def assemble(*halves):
        total = jnp.zeros((TILE, LANES), jnp.float32)
        for part, in_ref in enumerate(halves):
            for chunk in range(chunks):
                for group in range(groups):
                    rows = pl.ds(share * chunk + half * part + TILE * group, TILE)
                    for t, lanes in enumerate(columns):
                        number = (chunk * groups + group) * len(columns) + t
                        value = in_ref[pl.ds(2 * TILE * number, TILE), :]
                        scaled_ref[rows, lanes] = value
                        total = total + value * value
                        first = 2 * TILE * (TILE * group * len(columns) + t) + TILE + chunk
                        work_ref[rows, lanes] = in_ref[
                            pl.ds(first, TILE, stride=2 * TILE * len(columns)), :
                        ]
        total = jnp.sum(jnp.sum(total, axis=0, keepdims=True), axis=1, keepdims=True)
        inverse = 1.0 / jnp.sqrt(total + 1e-06)
        for first in range(0, width, LANES):
            rows = pl.ds(first, LANES)
            scaled_ref[rows, :] = scaled_ref[rows, :] * inverse + diagonal(first, DAMPING)

    def diagonal(first, value):
        row = lax.broadcasted_iota(jnp.int32, (LANES, width), 0)
        column = lax.broadcasted_iota(jnp.int32, (LANES, width), 1)
        return jnp.where(column == row + first, value, 0.0)

    def whole_product(right):
        for first in range(0, width, step):
            rows = pl.ds(first, step)
            left = [left_ref[number, rows, :] for number in range(3)]
            work_ref[rows, :] = product(left, lambda number: right[number], 3)

    def work(first):
        return work_ref[pl.ds(first, LANES), :]

    @pl.when(core_ref[0] == 0)
    def _():
        assemble(own_ref, other_ref)

    @pl.when(core_ref[0] != 0)
    def _():
        assemble(other_ref, own_ref)

    chosen = []
    for chunk in (y_ref[0], chunks - 1 - y_ref[0]):
        first = pl.multiple_of(share * chunk + half * core_ref[0], half)
        chosen.append(work_ref[pl.ds(first, half), :])
    chosen = jnp.concatenate(chosen, 0)

    for _ in range(2):
        cut_into(left_ref, 3, work)
        whole_product(left_ref)
    cut_into(left_ref, 3, work)
    cut_into(right_ref, 3, lambda first: scaled_ref[pl.ds(first, LANES), :])
    whole_product(right_ref)
    cut_into(left_ref, 2, lambda first: (diagonal(first, 5.0) - work(first)) * 0.25)
    estimate = product(cut(chosen, 2), lambda number: left_ref[number], 2)
    out_ref[...] = estimate

    @pl.when(count_ref[0] >= 2)
    def _():
        cut_into(right_ref, 2, work)
        rows = estimate
        for matrix in (left_ref, left_ref, left_ref, left_ref, right_ref):
            rows = product(cut(rows, 2), lambda number: matrix[number], 2)
        out_ref[...] = (5.0 * estimate - rows) * 0.25


def newton(core, y, count, own, other, width):
    square = (width, width)
    return pl.pallas_call(
        newton_kernel,
        out_shape=shape_of(width // TILE, width),
        in_specs=[SMEM] * 3 + [VMEM] * 2,
        out_specs=VMEM,
        scratch_shapes=[
            pltpu.VMEM(square, jnp.float32),
            pltpu.VMEM(square, jnp.float32),
            pltpu.VMEM((3,) + square, jnp.bfloat16),
            pltpu.VMEM((3,) + square, jnp.bfloat16),
        ],
        compiler_params=pltpu.CompilerParams(vmem_limit_bytes=14 * 1024 * 1024),
    )(core, y, count, own, other)


def local(grad, prev_stats, warm_roots, owner_items, counts, read_shard):
    gradients = grad[:, 0]
    width = gradients.shape[-1]
    kinds, lines = lax.axis_size("yh"), lax.axis_size("yl")
    y_count = kinds * lines
    kind = lax.axis_index("yh")
    y = kind * lines + lax.axis_index("yl")
    core = lax.axis_index("core")
    worker = lax.axis_index(WORKER)
    half = width // y_count // 2
    weight = (1.0 - HISTORY) / (y_count * 2 * gradients.shape[0])

    kept, sent = gram_halves(core.reshape(1), gradients, half, weight)
    got = lax.ppermute(sent, "core", SWAP)
    messages = build_messages(y.reshape(1), kept, got, prev_stats[0], warm_roots[0])
    peers = kept.shape[0]
    arrived = lax.all_to_all(messages.reshape(peers, 1, -1), PLANE, 0, 0, tiled=True)

    ids = jnp.arange(read_shard.shape[0], dtype=jnp.int32)
    blocks = jnp.sum(jnp.where(read_shard[None, :] == ids[:, None], ids[None, :], 0), 1)
    items = (2 * blocks[:, None] + jnp.arange(2, dtype=jnp.int32)).reshape(-1)
    matches = owner_items[None] == items[:, None, None]
    owners = jnp.sum(jnp.where(matches, ids[None, :, None], 0), (1, 2))
    slots = jnp.sum(jnp.where(matches, jnp.arange(2, dtype=jnp.int32), 0), (1, 2))
    mine = jnp.arange(counts.shape[0], dtype=jnp.int32) == 2 * blocks[worker] + kind
    iterations = jnp.sum(jnp.where(mine, counts, 0)).reshape(1)

    tiles = deliver(
        kind.reshape(1), blocks, owners, slots, arrived.reshape(messages.shape)
    )
    own = lax.all_to_all(tiles, LINE, 0, 0, tiled=True)
    other = lax.ppermute(own, "core", SWAP)
    root_rows = newton(
        core.reshape(1),
        y.reshape(1),
        iterations,
        own.reshape(-1, LANES),
        other.reshape(-1, LANES),
        width,
    )
    pairs = [(i, y_count - 1 - i) for i in range(y_count)]
    root_kept = root_rows[:half]
    root_got = lax.ppermute(root_rows[half:], ("yh", "yl"), pairs)
    result = jnp.where(
        kind == 0, jnp.stack([root_kept, root_got]), jnp.stack([root_got, root_kept])
    )
    return result[None]


def solution(mesh):
    kinds, cores, x_count = 2, 2, 4
    dp_count, worker_count = mesh.devices.shape
    chips = Mesh(
        mesh.devices.reshape(
            kinds, dp_count // (kinds * cores), cores, x_count, worker_count // x_count
        ),
        ("yh", "yl", "core", "x", "z"),
    )
    dp = ("yh", "yl", "core")
    return jax.shard_map(
        local,
        mesh=chips,
        in_specs=(
            P(dp, WORKER, None, None),
            P(WORKER, None, dp, None),
            P(WORKER, None, dp, None),
            P(),
            P(),
            P(),
        ),
        out_specs=P(WORKER, None, dp, None),
        check_vma=False,
    )
```

```python
import jax
import jax.numpy as jnp
from jax import lax
from jax.experimental import pallas as pl
from jax.experimental.pallas import tpu as pltpu
from jax.sharding import Mesh, PartitionSpec as P

HISTORY = 0.5
DAMPING = 0.001
WORKER = ("x", "z")
PLANE = ("yh", "yl", "x", "z")
LINE = ("yl", "x", "z")
SWAP = [(0, 1), (1, 0)]
LANES = 128
TILE = 8
EXTRA = 2
SMEM = pl.BlockSpec(memory_space=pltpu.SMEM)
VMEM = pl.BlockSpec(memory_space=pltpu.VMEM)
PARAMS = pltpu.CompilerParams(vmem_limit_bytes=8 * 1024 * 1024)


def shape_of(*shape):
    return jax.ShapeDtypeStruct(shape, jnp.float32)


def tile_columns(width):
    return [pl.ds(LANES * t, LANES) for t in range(width // LANES)]


def halves_kernel(weight, half, core_ref, grad_ref, kept_ref, sent_ref, gram_ref):
    core = core_ref[0]
    terms, width, _ = grad_ref.shape
    groups = half // TILE
    columns = tile_columns(width)
    chunks = width // (2 * half)
    count = chunks * groups * len(columns)
    step = 2 * LANES
    for kind in range(2):
        for first in range(0, width, step):
            part = pl.ds(first, step)
            total = jnp.zeros((step, width), jnp.float32)
            for term in range(terms):
                if kind == 0:
                    rows, axis = grad_ref[term, part, :], 1
                else:
                    rows, axis = grad_ref[term, :, part], 0
                total = total + lax.dot_general(
                    rows,
                    grad_ref[term],
                    (((axis,), (axis,)), ((), ())),
                    preferred_element_type=jnp.float32,
                )
            gram_ref[kind, part, :] = total * weight
    for out_ref, part in ((kept_ref, core), (sent_ref, 1 - core)):
        for kind in range(2):
            for chunk in range(chunks):
                for group in range(groups):
                    first = pl.multiple_of(2 * half * chunk + half * part + TILE * group, TILE)
                    for t, lanes in enumerate(columns):
                        number = (chunk * groups + group) * len(columns) + t + count * kind
                        out_ref[number] = gram_ref[kind, pl.ds(first, TILE), lanes]


def gram_halves(core, gradients, half, weight):
    width = gradients.shape[1]
    messages = width * width // (TILE * LANES)

    def kernel(*refs):
        halves_kernel(weight, half, *refs)

    return pl.pallas_call(
        kernel,
        out_shape=[shape_of(messages, TILE, LANES)] * 2,
        in_specs=[SMEM, VMEM],
        out_specs=[VMEM] * 2,
        scratch_shapes=[pltpu.VMEM((2, width, width), jnp.float32)],
        compiler_params=PARAMS,
    )(core, gradients)


def message_kernel(y_ref, kept_ref, got_ref, prev_ref, warm_ref, out_ref):
    _, rows, width = warm_ref.shape
    columns = tile_columns(width)
    size = TILE + EXTRA
    for number in range(kept_ref.shape[0]):
        out_ref[pl.ds(size * number, TILE), :] = kept_ref[number] + got_ref[number]
    count = kept_ref.shape[0] // 2
    shares = rows // TILE * len(columns)
    for kind in range(2):
        for part in range(shares):
            group, t = divmod(part, len(columns))
            number = count * kind + y_ref[0] * shares + part
            value = HISTORY * prev_ref[kind, pl.ds(TILE * group, TILE), columns[t]]
            out_ref[pl.ds(size * number, TILE), :] = kept_ref[number] + got_ref[number] + value
    for kind in range(2):
        for slot in range(EXTRA):
            for t, lanes in enumerate(columns):
                for first in range(0, rows, TILE):
                    number = (kind * rows + first) * len(columns) + t
                    out_ref[
                        pl.ds(size * number + TILE + slot, TILE, stride=size * len(columns)), :
                    ] = warm_ref[slot, pl.ds(first, TILE), lanes]


def build_messages(y, kept, got, prev, warm):
    return pl.pallas_call(
        message_kernel,
        out_shape=shape_of(kept.shape[0] * (TILE + EXTRA), LANES),
        in_specs=[SMEM] + [VMEM] * 4,
        out_specs=VMEM,
        compiler_params=PARAMS,
    )(y, kept, got, prev, warm)


def deliver_kernel(kind_ref, block_ref, owner_ref, slot_ref, in_ref, out_ref, dense_ref, sum_ref, warm_ref):
    kind = kind_ref[0]
    workers = block_ref.shape[0]
    size = TILE + EXTRA
    stride = workers * size
    chunks = in_ref.shape[0] // stride
    for first in range(0, stride, TILE):
        total = in_ref[pl.ds(first, TILE), :]
        for chunk in range(1, chunks):
            total = total + in_ref[pl.ds(first + stride * chunk, TILE), :]
        dense_ref[pl.ds(first, TILE), :] = total
    for worker in range(workers):
        sum_ref[worker] = dense_ref[pl.ds(size * worker, TILE), :]
        for slot in range(EXTRA):
            first = size * worker + TILE + slot
            warm_ref[EXTRA * worker + slot] = in_ref[pl.ds(first, chunks, stride=stride), :]
    for reader in range(workers):
        place = 2 * reader + kind
        sums = sum_ref[block_ref[reader]]
        warm = warm_ref[EXTRA * owner_ref[place] + slot_ref[place]]
        for number in range(reader, out_ref.shape[0], workers):
            out_ref[number, pl.ds(0, TILE), :] = sums
            out_ref[number, pl.ds(TILE, TILE), :] = warm


def deliver(kind, blocks, owners, slots, messages):
    workers = blocks.shape[0]
    rows = messages.shape[0]
    return pl.pallas_call(
        deliver_kernel,
        out_shape=shape_of(rows // (TILE + EXTRA) // 2, 2 * TILE, LANES),
        in_specs=[SMEM] * 4 + [VMEM],
        out_specs=VMEM,
        scratch_shapes=[
            pltpu.VMEM((workers * (TILE + EXTRA), LANES), jnp.float32),
            pltpu.VMEM((workers, TILE, LANES), jnp.float32),
            pltpu.VMEM((workers * EXTRA, TILE, LANES), jnp.float32),
        ],
        compiler_params=PARAMS,
    )(kind, blocks, owners, slots, messages)


def cut(value, parts):
    pieces = []
    for number in range(parts):
        piece = value.astype(jnp.bfloat16)
        pieces.append(piece)
        if number < parts - 1:
            value = value - piece.astype(jnp.float32)
    return pieces


def cut_into(out_ref, parts, first, value):
    rows = pl.ds(first, value.shape[0])
    for number, piece in enumerate(cut(value, parts)):
        out_ref[number, rows, :] = piece


def product(left, right, parts):
    total = None
    for order in reversed(range(parts)):
        for number in range(order + 1):
            term = jnp.dot(
                left[number], right(order - number), preferred_element_type=jnp.float32
            )
            total = term if total is None else total + term
    return total


def newton_kernel(
    core_ref, y_ref, count_ref, own_ref, other_ref, out_ref,
    stat_ref, work_ref, total_ref, first_ref, second_ref, third_ref
):
    width = stat_ref.shape[0]
    columns = tile_columns(width)
    chunks = TILE
    share = width // chunks
    half = share // 2
    groups = half // TILE
    step = 2 * LANES

    def assemble(*halves):
        total = jnp.zeros((TILE, LANES), jnp.float32)
        for part, in_ref in enumerate(halves):
            for chunk in range(chunks):
                for group in range(groups):
                    rows = pl.ds(share * chunk + half * part + TILE * group, TILE)
                    for t, lanes in enumerate(columns):
                        number = (chunk * groups + group) * len(columns) + t
                        value = in_ref[pl.ds(2 * TILE * number, TILE), :]
                        stat_ref[rows, lanes] = value
                        total = total + value * value
                        first = 2 * TILE * (TILE * group * len(columns) + t) + TILE + chunk
                        work_ref[rows, lanes] = in_ref[
                            pl.ds(first, TILE, stride=2 * TILE * len(columns)), :
                        ]
        total_ref[...] = total

    def diagonal(first, rows, value):
        row = lax.broadcasted_iota(jnp.int32, (rows, width), 0)
        column = lax.broadcasted_iota(jnp.int32, (rows, width), 1)
        return jnp.where(column == row + first, value, 0.0)

    def each_block(left_ref, right_ref, take):
        for first in range(0, width, step):
            rows = pl.ds(first, step)
            left = [left_ref[number, rows, :] for number in range(3)]
            take(first, product(left, lambda number: right_ref[number], 3))

    @pl.when(core_ref[0] == 0)
    def _():
        assemble(own_ref, other_ref)

    @pl.when(core_ref[0] != 0)
    def _():
        assemble(other_ref, own_ref)

    chosen = []
    for chunk in (y_ref[0], chunks - 1 - y_ref[0]):
        first = pl.multiple_of(share * chunk + half * core_ref[0], half)
        chosen.append(work_ref[pl.ds(first, half), :])
    chosen = jnp.concatenate(chosen, 0)

    for first in range(0, width, LANES):
        cut_into(first_ref, 3, first, work_ref[pl.ds(first, LANES), :])
    each_block(first_ref, first_ref, lambda first, value: cut_into(second_ref, 3, first, value))

    total = jnp.sum(jnp.sum(total_ref[...], axis=0, keepdims=True), axis=1, keepdims=True)
    inverse = 1.0 / jnp.sqrt(total + 1e-06)
    for first in range(0, width, LANES):
        value = stat_ref[pl.ds(first, LANES), :] * inverse + diagonal(first, LANES, DAMPING)
        cut_into(third_ref, 3, first, value)
    each_block(second_ref, second_ref, lambda first, value: cut_into(first_ref, 3, first, value))

    def take_coupled(first, value):
        work_ref[pl.ds(first, step), :] = value
        cut_into(second_ref, 2, first, (diagonal(first, step, 5.0) - value) * 0.25)

    each_block(first_ref, third_ref, take_coupled)
    estimate = product(cut(chosen, 2), lambda number: second_ref[number], 2)
    out_ref[...] = estimate

    @pl.when(count_ref[0] >= 2)
    def _():
        for first in range(0, width, LANES):
            cut_into(first_ref, 2, first, work_ref[pl.ds(first, LANES), :])
        rows = estimate
        for matrix in (second_ref, second_ref, second_ref, second_ref, first_ref):
            rows = product(cut(rows, 2), lambda number: matrix[number], 2)
        out_ref[...] = (5.0 * estimate - rows) * 0.25


def newton(core, y, count, own, other, width):
    square = (width, width)
    return pl.pallas_call(
        newton_kernel,
        out_shape=shape_of(width // TILE, width),
        in_specs=[SMEM] * 3 + [VMEM] * 2,
        out_specs=VMEM,
        scratch_shapes=[
            pltpu.VMEM(square, jnp.float32),
            pltpu.VMEM(square, jnp.float32),
            pltpu.VMEM((TILE, LANES), jnp.float32),
            pltpu.VMEM((3,) + square, jnp.bfloat16),
            pltpu.VMEM((3,) + square, jnp.bfloat16),
            pltpu.VMEM((3,) + square, jnp.bfloat16),
        ],
        compiler_params=pltpu.CompilerParams(vmem_limit_bytes=14 * 1024 * 1024),
    )(core, y, count, own, other)


def local(grad, prev_stats, warm_roots, owner_items, counts, read_shard):
    gradients = grad[:, 0]
    width = gradients.shape[-1]
    kinds, lines = lax.axis_size("yh"), lax.axis_size("yl")
    y_count = kinds * lines
    kind = lax.axis_index("yh")
    y = kind * lines + lax.axis_index("yl")
    core = lax.axis_index("core")
    worker = lax.axis_index(WORKER)
    half = width // y_count // 2
    weight = (1.0 - HISTORY) / (y_count * 2 * gradients.shape[0])

    kept, sent = gram_halves(core.reshape(1), gradients, half, weight)
    got = lax.ppermute(sent, "core", SWAP)
    messages = build_messages(y.reshape(1), kept, got, prev_stats[0], warm_roots[0])
    peers = kept.shape[0]
    arrived = lax.all_to_all(messages.reshape(peers, 1, -1), PLANE, 0, 0, tiled=True)

    ids = jnp.arange(read_shard.shape[0], dtype=jnp.int32)
    blocks = jnp.sum(jnp.where(read_shard[None, :] == ids[:, None], ids[None, :], 0), 1)
    items = (2 * blocks[:, None] + jnp.arange(2, dtype=jnp.int32)).reshape(-1)
    matches = owner_items[None] == items[:, None, None]
    owners = jnp.sum(jnp.where(matches, ids[None, :, None], 0), (1, 2))
    slots = jnp.sum(jnp.where(matches, jnp.arange(2, dtype=jnp.int32), 0), (1, 2))
    mine = jnp.arange(counts.shape[0], dtype=jnp.int32) == 2 * blocks[worker] + kind
    iterations = jnp.sum(jnp.where(mine, counts, 0)).reshape(1)

    tiles = deliver(
        kind.reshape(1), blocks, owners, slots, arrived.reshape(messages.shape)
    )
    own = lax.all_to_all(tiles, LINE, 0, 0, tiled=True)
    other = lax.ppermute(own, "core", SWAP)
    root_rows = newton(
        core.reshape(1),
        y.reshape(1),
        iterations,
        own.reshape(-1, LANES),
        other.reshape(-1, LANES),
        width,
    )
    pairs = [(i, y_count - 1 - i) for i in range(y_count)]
    root_kept = root_rows[:half]
    root_got = lax.ppermute(root_rows[half:], ("yh", "yl"), pairs)
    result = jnp.where(
        kind == 0, jnp.stack([root_kept, root_got]), jnp.stack([root_got, root_kept])
    )
    return result[None]


def solution(mesh):
    kinds, cores, x_count = 2, 2, 4
    dp_count, worker_count = mesh.devices.shape
    chips = Mesh(
        mesh.devices.reshape(
            kinds, dp_count // (kinds * cores), cores, x_count, worker_count // x_count
        ),
        ("yh", "yl", "core", "x", "z"),
    )
    dp = ("yh", "yl", "core")
    return jax.shard_map(
        local,
        mesh=chips,
        in_specs=(
            P(dp, WORKER, None, None),
            P(WORKER, None, dp, None),
            P(WORKER, None, dp, None),
            P(),
            P(),
            P(),
        ),
        out_specs=P(WORKER, None, dp, None),
        check_vma=False,
    )
```

```python
import jax
import jax.numpy as jnp
from jax import lax
from jax.experimental import pallas as pl
from jax.experimental.pallas import tpu as pltpu
from jax.sharding import Mesh, PartitionSpec as P

HISTORY = 0.5
DAMPING = 0.001
WORKER = ("x", "z")
PLANE = ("yh", "yl", "x", "z")
LINE = ("yl", "x", "z")
SWAP = [(0, 1), (1, 0)]
LANES = 128
TILE = 8
EXTRA = 2
SMEM = pl.BlockSpec(memory_space=pltpu.SMEM)
VMEM = pl.BlockSpec(memory_space=pltpu.VMEM)
PARAMS = pltpu.CompilerParams(vmem_limit_bytes=8 * 1024 * 1024)


def shape_of(*shape):
    return jax.ShapeDtypeStruct(shape, jnp.float32)


def tile_columns(width):
    return [pl.ds(LANES * t, LANES) for t in range(width // LANES)]


def halves_kernel(weight, half, core_ref, grad_ref, kept_ref, sent_ref, gram_ref):
    core = core_ref[0]
    terms, width, _ = grad_ref.shape
    groups = half // TILE
    columns = tile_columns(width)
    chunks = width // (2 * half)
    count = chunks * groups * len(columns)
    step = 2 * LANES
    for kind in range(2):
        for first in range(0, width, step):
            part = pl.ds(first, step)
            total = jnp.zeros((step, width), jnp.float32)
            for term in range(terms):
                if kind == 0:
                    rows, axis = grad_ref[term, part, :], 1
                else:
                    rows, axis = grad_ref[term, :, part], 0
                total = total + lax.dot_general(
                    rows,
                    grad_ref[term],
                    (((axis,), (axis,)), ((), ())),
                    preferred_element_type=jnp.float32,
                )
            gram_ref[kind, part, :] = total * weight
    for out_ref, part in ((kept_ref, core), (sent_ref, 1 - core)):
        for kind in range(2):
            for chunk in range(chunks):
                for group in range(groups):
                    first = pl.multiple_of(2 * half * chunk + half * part + TILE * group, TILE)
                    for t, lanes in enumerate(columns):
                        number = (chunk * groups + group) * len(columns) + t + count * kind
                        out_ref[number] = gram_ref[kind, pl.ds(first, TILE), lanes]


def gram_halves(core, gradients, half, weight):
    width = gradients.shape[1]
    messages = width * width // (TILE * LANES)

    def kernel(*refs):
        halves_kernel(weight, half, *refs)

    return pl.pallas_call(
        kernel,
        out_shape=[shape_of(messages, TILE, LANES)] * 2,
        in_specs=[SMEM, VMEM],
        out_specs=[VMEM] * 2,
        scratch_shapes=[pltpu.VMEM((2, width, width), jnp.float32)],
        compiler_params=PARAMS,
    )(core, gradients)


def message_kernel(y_ref, kept_ref, got_ref, prev_ref, warm_ref, out_ref):
    _, rows, width = warm_ref.shape
    columns = tile_columns(width)
    size = TILE + EXTRA
    for number in range(kept_ref.shape[0]):
        out_ref[pl.ds(size * number, TILE), :] = kept_ref[number] + got_ref[number]
    count = kept_ref.shape[0] // 2
    shares = rows // TILE * len(columns)
    for kind in range(2):
        for part in range(shares):
            group, t = divmod(part, len(columns))
            number = count * kind + y_ref[0] * shares + part
            value = HISTORY * prev_ref[kind, pl.ds(TILE * group, TILE), columns[t]]
            out_ref[pl.ds(size * number, TILE), :] = kept_ref[number] + got_ref[number] + value
    for kind in range(2):
        for slot in range(EXTRA):
            for t, lanes in enumerate(columns):
                for first in range(0, rows, TILE):
                    number = (kind * rows + first) * len(columns) + t
                    out_ref[
                        pl.ds(size * number + TILE + slot, TILE, stride=size * len(columns)), :
                    ] = warm_ref[slot, pl.ds(first, TILE), lanes]


def build_messages(y, kept, got, prev, warm):
    return pl.pallas_call(
        message_kernel,
        out_shape=shape_of(kept.shape[0] * (TILE + EXTRA), LANES),
        in_specs=[SMEM] + [VMEM] * 4,
        out_specs=VMEM,
        compiler_params=PARAMS,
    )(y, kept, got, prev, warm)


def deliver_kernel(kind_ref, block_ref, owner_ref, slot_ref, in_ref, out_ref, dense_ref, sum_ref, warm_ref):
    kind = kind_ref[0]
    workers = block_ref.shape[0]
    size = TILE + EXTRA
    stride = workers * size
    chunks = in_ref.shape[0] // stride
    for first in range(0, stride, TILE):
        total = in_ref[pl.ds(first, TILE), :]
        for chunk in range(1, chunks):
            total = total + in_ref[pl.ds(first + stride * chunk, TILE), :]
        dense_ref[pl.ds(first, TILE), :] = total
    for worker in range(workers):
        sum_ref[worker] = dense_ref[pl.ds(size * worker, TILE), :]
        for slot in range(EXTRA):
            first = size * worker + TILE + slot
            warm_ref[EXTRA * worker + slot] = in_ref[pl.ds(first, chunks, stride=stride), :]
    for reader in range(workers):
        place = 2 * reader + kind
        sums = sum_ref[block_ref[reader]]
        warm = warm_ref[EXTRA * owner_ref[place] + slot_ref[place]]
        for number in range(reader, out_ref.shape[0], workers):
            out_ref[number, pl.ds(0, TILE), :] = sums
            out_ref[number, pl.ds(TILE, TILE), :] = warm


def deliver(kind, blocks, owners, slots, messages):
    workers = blocks.shape[0]
    rows = messages.shape[0]
    return pl.pallas_call(
        deliver_kernel,
        out_shape=shape_of(rows // (TILE + EXTRA) // 2, 2 * TILE, LANES),
        in_specs=[SMEM] * 4 + [VMEM],
        out_specs=VMEM,
        scratch_shapes=[
            pltpu.VMEM((workers * (TILE + EXTRA), LANES), jnp.float32),
            pltpu.VMEM((workers, TILE, LANES), jnp.float32),
            pltpu.VMEM((workers * EXTRA, TILE, LANES), jnp.float32),
        ],
        compiler_params=PARAMS,
    )(kind, blocks, owners, slots, messages)


def cut(value, parts):
    pieces = []
    for number in range(parts):
        piece = value.astype(jnp.bfloat16)
        pieces.append(piece)
        if number < parts - 1:
            value = value - piece.astype(jnp.float32)
    return pieces


def cut_left(out_ref, parts, first, value):
    rows, width = value.shape
    for number, piece in enumerate(cut(value, parts)):
        out_ref[pl.ds(first, rows), pl.ds(width * number, width)] = piece


def cut_right(out_ref, parts, first, value):
    rows, width = value.shape
    for number, piece in enumerate(cut(value, parts)):
        out_ref[pl.ds(width * (parts - 1 - number) + first, rows), :] = piece


def product(left_of, right_ref, parts):
    width = right_ref.shape[1]
    total = None
    for count in reversed(range(1, parts + 1)):
        term = jnp.dot(
            left_of(width * count),
            right_ref[pl.ds(width * (parts - count), width * count), :],
            preferred_element_type=jnp.float32,
        )
        total = term if total is None else total + term
    return total


def newton_kernel(
    core_ref, y_ref, count_ref, own_ref, other_ref, out_ref,
    stat_ref, work_ref, total_ref, left_ref, next_ref, right_ref, square_ref, scaled_ref
):
    width = stat_ref.shape[0]
    columns = tile_columns(width)
    chunks = TILE
    share = width // chunks
    half = share // 2
    groups = half // TILE
    step = 2 * LANES

    def assemble(*halves):
        total = jnp.zeros((TILE, LANES), jnp.float32)
        for part, in_ref in enumerate(halves):
            for chunk in range(chunks):
                for group in range(groups):
                    rows = pl.ds(share * chunk + half * part + TILE * group, TILE)
                    for t, lanes in enumerate(columns):
                        number = (chunk * groups + group) * len(columns) + t
                        value = in_ref[pl.ds(2 * TILE * number, TILE), :]
                        stat_ref[rows, lanes] = value
                        total = total + value * value
                        first = 2 * TILE * (TILE * group * len(columns) + t) + TILE + chunk
                        work_ref[rows, lanes] = in_ref[
                            pl.ds(first, TILE, stride=2 * TILE * len(columns)), :
                        ]
        total_ref[...] = total

    def diagonal(first, rows, value):
        row = lax.broadcasted_iota(jnp.int32, (rows, width), 0)
        column = lax.broadcasted_iota(jnp.int32, (rows, width), 1)
        return jnp.where(column == row + first, value, 0.0)

    def each_block(left_ref, right_ref, take):
        for first in range(0, width, step):
            rows = pl.ds(first, step)
            take(first, product(lambda terms: left_ref[rows, pl.ds(0, terms)], right_ref, 3))

    def row_product(rows, right_ref):
        pieces = jnp.concatenate(cut(rows, 2), 1)
        return product(lambda terms: pieces[:, :terms], right_ref, 2)

    @pl.when(core_ref[0] == 0)
    def _():
        assemble(own_ref, other_ref)

    @pl.when(core_ref[0] != 0)
    def _():
        assemble(other_ref, own_ref)

    chosen = []
    for chunk in (y_ref[0], chunks - 1 - y_ref[0]):
        first = pl.multiple_of(share * chunk + half * core_ref[0], half)
        chosen.append(work_ref[pl.ds(first, half), :])
    chosen = jnp.concatenate(chosen, 0)

    for first in range(0, width, LANES):
        value = work_ref[pl.ds(first, LANES), :]
        cut_left(left_ref, 3, first, value)
        cut_right(right_ref, 3, first, value)

    def take_square(first, value):
        cut_left(next_ref, 3, first, value)
        cut_right(square_ref, 3, first, value)

    each_block(left_ref, right_ref, take_square)

    total = jnp.sum(jnp.sum(total_ref[...], axis=0, keepdims=True), axis=1, keepdims=True)
    inverse = 1.0 / jnp.sqrt(total + 1e-06)
    for first in range(0, width, LANES):
        value = stat_ref[pl.ds(first, LANES), :] * inverse + diagonal(first, LANES, DAMPING)
        cut_right(scaled_ref, 3, first, value)
    each_block(next_ref, square_ref, lambda first, value: cut_left(left_ref, 3, first, value))

    def take_coupled(first, value):
        work_ref[pl.ds(first, step), :] = value
        cut_right(right_ref, 2, first, (diagonal(first, step, 5.0) - value) * 0.25)

    each_block(left_ref, scaled_ref, take_coupled)
    factor_ref = right_ref.at[pl.ds(0, 2 * width)]
    estimate = row_product(chosen, factor_ref)
    out_ref[...] = estimate

    @pl.when(count_ref[0] >= 2)
    def _():
        for first in range(0, width, LANES):
            cut_right(square_ref, 2, first, work_ref[pl.ds(first, LANES), :])
        coupled_ref = square_ref.at[pl.ds(0, 2 * width)]
        rows = estimate
        for matrix in (factor_ref, factor_ref, factor_ref, factor_ref, coupled_ref):
            rows = row_product(rows, matrix)
        out_ref[...] = (5.0 * estimate - rows) * 0.25


def newton(core, y, count, own, other, width):
    square = (width, width)
    return pl.pallas_call(
        newton_kernel,
        out_shape=shape_of(width // TILE, width),
        in_specs=[SMEM] * 3 + [VMEM] * 2,
        out_specs=VMEM,
        scratch_shapes=[
            pltpu.VMEM(square, jnp.float32),
            pltpu.VMEM(square, jnp.float32),
            pltpu.VMEM((TILE, LANES), jnp.float32),
            pltpu.VMEM((width, 3 * width), jnp.bfloat16),
            pltpu.VMEM((width, 3 * width), jnp.bfloat16),
            pltpu.VMEM((3 * width, width), jnp.bfloat16),
            pltpu.VMEM((3 * width, width), jnp.bfloat16),
            pltpu.VMEM((3 * width, width), jnp.bfloat16),
        ],
        compiler_params=pltpu.CompilerParams(vmem_limit_bytes=16 * 1024 * 1024),
    )(core, y, count, own, other)


def local(grad, prev_stats, warm_roots, owner_items, counts, read_shard):
    gradients = grad[:, 0]
    width = gradients.shape[-1]
    kinds, lines = lax.axis_size("yh"), lax.axis_size("yl")
    y_count = kinds * lines
    kind = lax.axis_index("yh")
    y = kind * lines + lax.axis_index("yl")
    core = lax.axis_index("core")
    worker = lax.axis_index(WORKER)
    half = width // y_count // 2
    weight = (1.0 - HISTORY) / (y_count * 2 * gradients.shape[0])

    kept, sent = gram_halves(core.reshape(1), gradients, half, weight)
    got = lax.ppermute(sent, "core", SWAP)
    messages = build_messages(y.reshape(1), kept, got, prev_stats[0], warm_roots[0])
    peers = kept.shape[0]
    arrived = lax.all_to_all(messages.reshape(peers, 1, -1), PLANE, 0, 0, tiled=True)

    ids = jnp.arange(read_shard.shape[0], dtype=jnp.int32)
    blocks = jnp.sum(jnp.where(read_shard[None, :] == ids[:, None], ids[None, :], 0), 1)
    items = (2 * blocks[:, None] + jnp.arange(2, dtype=jnp.int32)).reshape(-1)
    matches = owner_items[None] == items[:, None, None]
    owners = jnp.sum(jnp.where(matches, ids[None, :, None], 0), (1, 2))
    slots = jnp.sum(jnp.where(matches, jnp.arange(2, dtype=jnp.int32), 0), (1, 2))
    mine = jnp.arange(counts.shape[0], dtype=jnp.int32) == 2 * blocks[worker] + kind
    iterations = jnp.sum(jnp.where(mine, counts, 0)).reshape(1)

    tiles = deliver(
        kind.reshape(1), blocks, owners, slots, arrived.reshape(messages.shape)
    )
    own = lax.all_to_all(tiles, LINE, 0, 0, tiled=True)
    other = lax.ppermute(own, "core", SWAP)
    root_rows = newton(
        core.reshape(1),
        y.reshape(1),
        iterations,
        own.reshape(-1, LANES),
        other.reshape(-1, LANES),
        width,
    )
    pairs = [(i, y_count - 1 - i) for i in range(y_count)]
    root_kept = root_rows[:half]
    root_got = lax.ppermute(root_rows[half:], ("yh", "yl"), pairs)
    result = jnp.where(
        kind == 0, jnp.stack([root_kept, root_got]), jnp.stack([root_got, root_kept])
    )
    return result[None]


def solution(mesh):
    kinds, cores, x_count = 2, 2, 4
    dp_count, worker_count = mesh.devices.shape
    chips = Mesh(
        mesh.devices.reshape(
            kinds, dp_count // (kinds * cores), cores, x_count, worker_count // x_count
        ),
        ("yh", "yl", "core", "x", "z"),
    )
    dp = ("yh", "yl", "core")
    return jax.shard_map(
        local,
        mesh=chips,
        in_specs=(
            P(dp, WORKER, None, None),
            P(WORKER, None, dp, None),
            P(WORKER, None, dp, None),
            P(),
            P(),
            P(),
        ),
        out_specs=P(WORKER, None, dp, None),
        check_vma=False,
    )
```

```python
import jax
import jax.numpy as jnp
from jax import lax
from jax.experimental import pallas as pl
from jax.experimental.pallas import tpu as pltpu
from jax.sharding import Mesh, PartitionSpec as P

HISTORY = 0.5
DAMPING = 0.001
WORKER = ("x", "z")
PLANE = ("yh", "yl", "z", "x")
LINE = ("yl", "z", "x")
SWAP = [(0, 1), (1, 0)]
LANES = 128
TILE = 8
EXTRA = 2
SMEM = pl.BlockSpec(memory_space=pltpu.SMEM)
VMEM = pl.BlockSpec(memory_space=pltpu.VMEM)
PARAMS = pltpu.CompilerParams(vmem_limit_bytes=8 * 1024 * 1024)


def shape_of(*shape):
    return jax.ShapeDtypeStruct(shape, jnp.float32)


def tile_columns(width):
    return [pl.ds(LANES * t, LANES) for t in range(width // LANES)]


def halves_kernel(weight, half, core_ref, grad_ref, kept_ref, sent_ref, gram_ref):
    core = core_ref[0]
    terms, width, _ = grad_ref.shape
    groups = half // TILE
    columns = tile_columns(width)
    chunks = width // (2 * half)
    count = chunks * groups * len(columns)
    step = 2 * LANES
    for kind in range(2):
        for first in range(0, width, step):
            part = pl.ds(first, step)
            total = jnp.zeros((step, width), jnp.float32)
            for term in range(terms):
                if kind == 0:
                    rows, axis = grad_ref[term, part, :], 1
                else:
                    rows, axis = grad_ref[term, :, part], 0
                total = total + lax.dot_general(
                    rows,
                    grad_ref[term],
                    (((axis,), (axis,)), ((), ())),
                    preferred_element_type=jnp.float32,
                )
            gram_ref[kind, part, :] = total * weight
    for out_ref, part in ((kept_ref, core), (sent_ref, 1 - core)):
        for kind in range(2):
            for chunk in range(chunks):
                for group in range(groups):
                    first = pl.multiple_of(2 * half * chunk + half * part + TILE * group, TILE)
                    for t, lanes in enumerate(columns):
                        number = (chunk * groups + group) * len(columns) + t + count * kind
                        out_ref[number] = gram_ref[kind, pl.ds(first, TILE), lanes]


def gram_halves(core, gradients, half, weight):
    width = gradients.shape[1]
    messages = width * width // (TILE * LANES)

    def kernel(*refs):
        halves_kernel(weight, half, *refs)

    return pl.pallas_call(
        kernel,
        out_shape=[shape_of(messages, TILE, LANES)] * 2,
        in_specs=[SMEM, VMEM],
        out_specs=[VMEM] * 2,
        scratch_shapes=[pltpu.VMEM((2, width, width), jnp.float32)],
        compiler_params=PARAMS,
    )(core, gradients)


def message_kernel(y_ref, kept_ref, got_ref, prev_ref, warm_ref, out_ref):
    _, rows, width = warm_ref.shape
    columns = tile_columns(width)
    size = TILE + EXTRA
    for number in range(kept_ref.shape[0]):
        out_ref[pl.ds(size * number, TILE), :] = kept_ref[number] + got_ref[number]
    count = kept_ref.shape[0] // 2
    shares = rows // TILE * len(columns)
    for kind in range(2):
        for part in range(shares):
            group, t = divmod(part, len(columns))
            number = count * kind + y_ref[0] * shares + part
            value = HISTORY * prev_ref[kind, pl.ds(TILE * group, TILE), columns[t]]
            out_ref[pl.ds(size * number, TILE), :] = kept_ref[number] + got_ref[number] + value
    for kind in range(2):
        for slot in range(EXTRA):
            for t, lanes in enumerate(columns):
                for first in range(0, rows, TILE):
                    number = (kind * rows + first) * len(columns) + t
                    out_ref[
                        pl.ds(size * number + TILE + slot, TILE, stride=size * len(columns)), :
                    ] = warm_ref[slot, pl.ds(first, TILE), lanes]


def build_messages(y, kept, got, prev, warm):
    return pl.pallas_call(
        message_kernel,
        out_shape=shape_of(kept.shape[0] * (TILE + EXTRA), LANES),
        in_specs=[SMEM] + [VMEM] * 4,
        out_specs=VMEM,
        compiler_params=PARAMS,
    )(y, kept, got, prev, warm)


def deliver_kernel(kind_ref, block_ref, owner_ref, slot_ref, in_ref, out_ref, dense_ref, sum_ref, warm_ref):
    kind = kind_ref[0]
    workers = block_ref.shape[0]
    size = TILE + EXTRA
    stride = workers * size
    chunks = in_ref.shape[0] // stride
    for first in range(0, stride, TILE):
        total = in_ref[pl.ds(first, TILE), :]
        for chunk in range(1, chunks):
            total = total + in_ref[pl.ds(first + stride * chunk, TILE), :]
        dense_ref[pl.ds(first, TILE), :] = total
    for worker in range(workers):
        sum_ref[worker] = dense_ref[pl.ds(size * worker, TILE), :]
        for slot in range(EXTRA):
            first = size * worker + TILE + slot
            warm_ref[EXTRA * worker + slot] = in_ref[pl.ds(first, chunks, stride=stride), :]
    for reader in range(workers):
        place = 2 * reader + kind
        sums = sum_ref[block_ref[reader]]
        warm = warm_ref[EXTRA * owner_ref[place] + slot_ref[place]]
        for number in range(reader, out_ref.shape[0], workers):
            out_ref[number, pl.ds(0, TILE), :] = sums
            out_ref[number, pl.ds(TILE, TILE), :] = warm


def deliver(kind, blocks, owners, slots, messages):
    workers = blocks.shape[0]
    rows = messages.shape[0]
    return pl.pallas_call(
        deliver_kernel,
        out_shape=shape_of(rows // (TILE + EXTRA) // 2, 2 * TILE, LANES),
        in_specs=[SMEM] * 4 + [VMEM],
        out_specs=VMEM,
        scratch_shapes=[
            pltpu.VMEM((workers * (TILE + EXTRA), LANES), jnp.float32),
            pltpu.VMEM((workers, TILE, LANES), jnp.float32),
            pltpu.VMEM((workers * EXTRA, TILE, LANES), jnp.float32),
        ],
        compiler_params=PARAMS,
    )(kind, blocks, owners, slots, messages)


def cut(value, parts):
    pieces = []
    for number in range(parts):
        piece = value.astype(jnp.bfloat16)
        pieces.append(piece)
        if number < parts - 1:
            value = value - piece.astype(jnp.float32)
    return pieces


def cut_left(out_ref, parts, first, value):
    rows, width = value.shape
    for number, piece in enumerate(cut(value, parts)):
        out_ref[pl.ds(first, rows), pl.ds(width * number, width)] = piece


def cut_right(out_ref, parts, first, value):
    rows, width = value.shape
    for number, piece in enumerate(cut(value, parts)):
        out_ref[pl.ds(width * (parts - 1 - number) + first, rows), :] = piece


def product(left_of, right_ref, parts):
    width = right_ref.shape[1]
    total = None
    for count in reversed(range(1, parts + 1)):
        term = jnp.dot(
            left_of(width * count),
            right_ref[pl.ds(width * (parts - count), width * count), :],
            preferred_element_type=jnp.float32,
        )
        total = term if total is None else total + term
    return total


def newton_kernel(
    core_ref, y_ref, count_ref, own_ref, other_ref, out_ref,
    stat_ref, work_ref, total_ref, left_ref, next_ref, right_ref, square_ref, scaled_ref
):
    width = stat_ref.shape[0]
    columns = tile_columns(width)
    chunks = TILE
    share = width // chunks
    half = share // 2
    groups = half // TILE
    step = 2 * LANES

    def assemble(*halves):
        total = jnp.zeros((TILE, LANES), jnp.float32)
        for part, in_ref in enumerate(halves):
            for chunk in range(chunks):
                for group in range(groups):
                    rows = pl.ds(share * chunk + half * part + TILE * group, TILE)
                    for t, lanes in enumerate(columns):
                        number = (chunk * groups + group) * len(columns) + t
                        value = in_ref[pl.ds(2 * TILE * number, TILE), :]
                        stat_ref[rows, lanes] = value
                        total = total + value * value
                        first = 2 * TILE * (TILE * group * len(columns) + t) + TILE + chunk
                        work_ref[rows, lanes] = in_ref[
                            pl.ds(first, TILE, stride=2 * TILE * len(columns)), :
                        ]
        total_ref[...] = total

    def diagonal(first, rows, value):
        row = lax.broadcasted_iota(jnp.int32, (rows, width), 0)
        column = lax.broadcasted_iota(jnp.int32, (rows, width), 1)
        return jnp.where(column == row + first, value, 0.0)

    def each_block(left_ref, right_ref, take):
        for first in range(0, width, step):
            rows = pl.ds(first, step)
            take(first, product(lambda terms: left_ref[rows, pl.ds(0, terms)], right_ref, 3))

    def row_product(rows, right_ref):
        pieces = jnp.concatenate(cut(rows, 2), 1)
        return product(lambda terms: pieces[:, :terms], right_ref, 2)

    @pl.when(core_ref[0] == 0)
    def _():
        assemble(own_ref, other_ref)

    @pl.when(core_ref[0] != 0)
    def _():
        assemble(other_ref, own_ref)

    chosen = []
    for chunk in (y_ref[0], chunks - 1 - y_ref[0]):
        first = pl.multiple_of(share * chunk + half * core_ref[0], half)
        chosen.append(work_ref[pl.ds(first, half), :])
    chosen = jnp.concatenate(chosen, 0)

    for first in range(0, width, LANES):
        value = work_ref[pl.ds(first, LANES), :]
        cut_left(left_ref, 3, first, value)
        cut_right(right_ref, 3, first, value)

    def take_square(first, value):
        cut_left(next_ref, 3, first, value)
        cut_right(square_ref, 3, first, value)

    each_block(left_ref, right_ref, take_square)

    total = jnp.sum(jnp.sum(total_ref[...], axis=0, keepdims=True), axis=1, keepdims=True)
    inverse = 1.0 / jnp.sqrt(total + 1e-06)
    for first in range(0, width, LANES):
        value = stat_ref[pl.ds(first, LANES), :] * inverse + diagonal(first, LANES, DAMPING)
        cut_right(scaled_ref, 3, first, value)
    each_block(next_ref, square_ref, lambda first, value: cut_left(left_ref, 3, first, value))

    def take_coupled(first, value):
        work_ref[pl.ds(first, step), :] = value
        cut_right(right_ref, 2, first, (diagonal(first, step, 5.0) - value) * 0.25)

    each_block(left_ref, scaled_ref, take_coupled)
    factor_ref = right_ref.at[pl.ds(0, 2 * width)]
    estimate = row_product(chosen, factor_ref)
    out_ref[...] = estimate

    @pl.when(count_ref[0] >= 2)
    def _():
        for first in range(0, width, LANES):
            cut_right(square_ref, 2, first, work_ref[pl.ds(first, LANES), :])
        coupled_ref = square_ref.at[pl.ds(0, 2 * width)]
        rows = estimate
        for matrix in (factor_ref, factor_ref, factor_ref, factor_ref, coupled_ref):
            rows = row_product(rows, matrix)
        out_ref[...] = (5.0 * estimate - rows) * 0.25


def newton(core, y, count, own, other, width):
    square = (width, width)
    return pl.pallas_call(
        newton_kernel,
        out_shape=shape_of(width // TILE, width),
        in_specs=[SMEM] * 3 + [VMEM] * 2,
        out_specs=VMEM,
        scratch_shapes=[
            pltpu.VMEM(square, jnp.float32),
            pltpu.VMEM(square, jnp.float32),
            pltpu.VMEM((TILE, LANES), jnp.float32),
            pltpu.VMEM((width, 3 * width), jnp.bfloat16),
            pltpu.VMEM((width, 3 * width), jnp.bfloat16),
            pltpu.VMEM((3 * width, width), jnp.bfloat16),
            pltpu.VMEM((3 * width, width), jnp.bfloat16),
            pltpu.VMEM((3 * width, width), jnp.bfloat16),
        ],
        compiler_params=pltpu.CompilerParams(vmem_limit_bytes=16 * 1024 * 1024),
    )(core, y, count, own, other)


def local(grad, prev_stats, warm_roots, owner_items, counts, read_shard):
    gradients = grad[:, 0]
    width = gradients.shape[-1]
    kinds, lines = lax.axis_size("yh"), lax.axis_size("yl")
    y_count = kinds * lines
    kind = lax.axis_index("yh")
    y = kind * lines + lax.axis_index("yl")
    core = lax.axis_index("core")
    worker = lax.axis_index(WORKER)
    half = width // y_count // 2
    weight = (1.0 - HISTORY) / (y_count * 2 * gradients.shape[0])

    kept, sent = gram_halves(core.reshape(1), gradients, half, weight)
    got = lax.ppermute(sent, "core", SWAP)
    messages = build_messages(y.reshape(1), kept, got, prev_stats[0], warm_roots[0])
    peers = kept.shape[0]
    arrived = lax.all_to_all(messages.reshape(peers, 1, -1), PLANE, 0, 0, tiled=True)

    ids = jnp.arange(read_shard.shape[0], dtype=jnp.int32)
    blocks = jnp.sum(jnp.where(read_shard[None, :] == ids[:, None], ids[None, :], 0), 1)
    items = (2 * blocks[:, None] + jnp.arange(2, dtype=jnp.int32)).reshape(-1)
    matches = owner_items[None] == items[:, None, None]
    owners = jnp.sum(jnp.where(matches, ids[None, :, None], 0), (1, 2))
    slots = jnp.sum(jnp.where(matches, jnp.arange(2, dtype=jnp.int32), 0), (1, 2))
    mine = jnp.arange(counts.shape[0], dtype=jnp.int32) == 2 * blocks[worker] + kind
    iterations = jnp.sum(jnp.where(mine, counts, 0)).reshape(1)

    x_count, z_count = lax.axis_size("x"), lax.axis_size("z")

    def place_of(number):
        return number % z_count * x_count + number // z_count

    def in_place(values):
        return values.reshape(x_count, z_count, -1).transpose(1, 0, 2).reshape(-1)

    block_places = in_place(place_of(blocks))
    owner_places = in_place(place_of(owners))

    tiles = deliver(
        kind.reshape(1), block_places, owner_places, in_place(slots), arrived.reshape(messages.shape)
    )
    own = lax.all_to_all(tiles, LINE, 0, 0, tiled=True)
    other = lax.ppermute(own, "core", SWAP)
    root_rows = newton(
        core.reshape(1),
        y.reshape(1),
        iterations,
        own.reshape(-1, LANES),
        other.reshape(-1, LANES),
        width,
    )
    pairs = [(i, y_count - 1 - i) for i in range(y_count)]
    root_kept = root_rows[:half]
    root_got = lax.ppermute(root_rows[half:], ("yh", "yl"), pairs)
    result = jnp.where(
        kind == 0, jnp.stack([root_kept, root_got]), jnp.stack([root_got, root_kept])
    )
    return result[None]


def solution(mesh):
    kinds, cores, x_count = 2, 2, 4
    dp_count, worker_count = mesh.devices.shape
    chips = Mesh(
        mesh.devices.reshape(
            kinds, dp_count // (kinds * cores), cores, x_count, worker_count // x_count
        ),
        ("yh", "yl", "core", "x", "z"),
    )
    dp = ("yh", "yl", "core")
    return jax.shard_map(
        local,
        mesh=chips,
        in_specs=(
            P(dp, WORKER, None, None),
            P(WORKER, None, dp, None),
            P(WORKER, None, dp, None),
            P(),
            P(),
            P(),
        ),
        out_specs=P(WORKER, None, dp, None),
        check_vma=False,
    )
```

```python
import jax
import jax.numpy as jnp
from jax import lax
from jax.experimental import pallas as pl
from jax.experimental.pallas import tpu as pltpu
from jax.sharding import Mesh, PartitionSpec as P

HISTORY = 0.5
DAMPING = 0.001
WORKER = ("x", "z")
PLANE = ("x", "yh", "yl", "z")
LINE = ("x", "yl", "z")
SWAP = [(0, 1), (1, 0)]
LANES = 128
TILE = 8
EXTRA = 2
DEPTH = 8
LINES = 4
SMEM = pl.BlockSpec(memory_space=pltpu.SMEM)
VMEM = pl.BlockSpec(memory_space=pltpu.VMEM)
PARAMS = pltpu.CompilerParams(vmem_limit_bytes=8 * 1024 * 1024)


def shape_of(*shape):
    return jax.ShapeDtypeStruct(shape, jnp.float32)


def tile_columns(width):
    return [pl.ds(LANES * t, LANES) for t in range(width // LANES)]


def halves_kernel(weight, half, core_ref, grad_ref, kept_ref, sent_ref, gram_ref):
    core = core_ref[0]
    terms, width, _ = grad_ref.shape
    groups = half // TILE
    columns = tile_columns(width)
    chunks = width // (2 * half)
    count = chunks * groups * len(columns)
    step = 2 * LANES
    for kind in range(2):
        for first in range(0, width, step):
            part = pl.ds(first, step)
            total = jnp.zeros((step, width), jnp.float32)
            for term in range(terms):
                if kind == 0:
                    rows, axis = grad_ref[term, part, :], 1
                else:
                    rows, axis = grad_ref[term, :, part], 0
                total = total + lax.dot_general(
                    rows,
                    grad_ref[term],
                    (((axis,), (axis,)), ((), ())),
                    preferred_element_type=jnp.float32,
                )
            gram_ref[kind, part, :] = total * weight
    for out_ref, part in ((kept_ref, core), (sent_ref, 1 - core)):
        for kind in range(2):
            for chunk in range(chunks):
                for group in range(groups):
                    first = pl.multiple_of(2 * half * chunk + half * part + TILE * group, TILE)
                    for t, lanes in enumerate(columns):
                        number = (chunk * groups + group) * len(columns) + t + count * kind
                        out_ref[number] = gram_ref[kind, pl.ds(first, TILE), lanes]


def gram_halves(core, gradients, half, weight):
    width = gradients.shape[1]
    messages = width * width // (TILE * LANES)

    def kernel(*refs):
        halves_kernel(weight, half, *refs)

    return pl.pallas_call(
        kernel,
        out_shape=[shape_of(messages, TILE, LANES)] * 2,
        in_specs=[SMEM, VMEM],
        out_specs=[VMEM] * 2,
        scratch_shapes=[pltpu.VMEM((2, width, width), jnp.float32)],
        compiler_params=PARAMS,
    )(core, gradients)


def message_place(number, chunks):
    columns = 4
    chunk, piece = divmod(number, columns * DEPTH)
    return (piece % columns * chunks + chunk) * DEPTH + piece // columns


def message_kernel(y_ref, kept_ref, got_ref, prev_ref, warm_ref, out_ref):
    _, rows, width = warm_ref.shape
    columns = tile_columns(width)
    size = TILE + EXTRA
    for number in range(kept_ref.shape[0]):
        first = size * message_place(number, TILE)
        out_ref[pl.ds(first, TILE), :] = kept_ref[number] + got_ref[number]
    count = kept_ref.shape[0] // 2
    shares = rows // TILE * len(columns)
    for kind in range(2):
        for part in range(shares):
            group, t = divmod(part, len(columns))
            number = count * kind + y_ref[0] * shares + part
            value = HISTORY * prev_ref[kind, pl.ds(TILE * group, TILE), columns[t]]
            line = DEPTH * (2 * LINES * t + LINES * kind) + LINES * y_ref[0] + group
            out_ref[pl.ds(size * line, TILE), :] = kept_ref[number] + got_ref[number] + value
    for kind in range(2):
        for slot in range(EXTRA):
            for t, lanes in enumerate(columns):
                for first in range(0, rows, TILE):
                    line = DEPTH * (2 * LINES * t + LINES * kind + first // TILE)
                    out_ref[
                        pl.ds(size * line + TILE + slot, TILE, stride=size), :
                    ] = warm_ref[slot, pl.ds(first, TILE), lanes]


def build_messages(y, kept, got, prev, warm):
    return pl.pallas_call(
        message_kernel,
        out_shape=shape_of(kept.shape[0] * (TILE + EXTRA), LANES),
        in_specs=[SMEM] + [VMEM] * 4,
        out_specs=VMEM,
        compiler_params=PARAMS,
    )(y, kept, got, prev, warm)


def deliver_kernel(kind_ref, block_ref, owner_ref, slot_ref, in_ref, out_ref, sum_ref, warm_ref):
    kind = kind_ref[0]
    workers = block_ref.shape[0]
    size = TILE + EXTRA
    chunks = in_ref.shape[0] // (workers * size)
    stride = DEPTH * size
    for worker in range(workers):
        base = size * (worker // DEPTH * chunks * DEPTH + worker % DEPTH)
        total = in_ref[pl.ds(base, TILE), :]
        for chunk in range(1, chunks):
            total = total + in_ref[pl.ds(base + stride * chunk, TILE), :]
        sum_ref[worker] = total
        for slot in range(EXTRA):
            first = base + TILE + slot
            warm_ref[EXTRA * worker + slot] = in_ref[pl.ds(first, chunks, stride=stride), :]
    for reader in range(workers):
        place = 2 * reader + kind
        sums = sum_ref[block_ref[reader]]
        warm = warm_ref[EXTRA * owner_ref[place] + slot_ref[place]]
        for line in range(LINES):
            number = (reader // DEPTH * LINES + line) * DEPTH + reader % DEPTH
            out_ref[number, pl.ds(0, TILE), :] = sums
            out_ref[number, pl.ds(TILE, TILE), :] = warm


def deliver(kind, blocks, owners, slots, messages):
    workers = blocks.shape[0]
    rows = messages.shape[0]
    return pl.pallas_call(
        deliver_kernel,
        out_shape=shape_of(rows // (TILE + EXTRA) // 2, 2 * TILE, LANES),
        in_specs=[SMEM] * 4 + [VMEM],
        out_specs=VMEM,
        scratch_shapes=[
            pltpu.VMEM((workers, TILE, LANES), jnp.float32),
            pltpu.VMEM((workers * EXTRA, TILE, LANES), jnp.float32),
        ],
        compiler_params=PARAMS,
    )(kind, blocks, owners, slots, messages)


def cut(value, parts):
    pieces = []
    for number in range(parts):
        piece = value.astype(jnp.bfloat16)
        pieces.append(piece)
        if number < parts - 1:
            value = value - piece.astype(jnp.float32)
    return pieces


def cut_left(out_ref, parts, first, value):
    rows, width = value.shape
    for number, piece in enumerate(cut(value, parts)):
        out_ref[pl.ds(first, rows), pl.ds(width * number, width)] = piece


def cut_right(out_ref, parts, first, value):
    rows, width = value.shape
    for number, piece in enumerate(cut(value, parts)):
        out_ref[pl.ds(width * (parts - 1 - number) + first, rows), :] = piece


def product(left_of, right_ref, parts):
    width = right_ref.shape[1]
    total = None
    for count in reversed(range(1, parts + 1)):
        term = jnp.dot(
            left_of(width * count),
            right_ref[pl.ds(width * (parts - count), width * count), :],
            preferred_element_type=jnp.float32,
        )
        total = term if total is None else total + term
    return total


def newton_kernel(
    core_ref, y_ref, count_ref, own_ref, other_ref, out_ref,
    stat_ref, work_ref, total_ref, left_ref, next_ref, right_ref, square_ref, scaled_ref
):
    width = stat_ref.shape[0]
    columns = tile_columns(width)
    chunks = TILE
    share = width // chunks
    half = share // 2
    groups = half // TILE
    step = 2 * LANES

    def assemble(*halves):
        total = jnp.zeros((TILE, LANES), jnp.float32)
        for part, in_ref in enumerate(halves):
            for chunk in range(chunks):
                for group in range(groups):
                    rows = pl.ds(share * chunk + half * part + TILE * group, TILE)
                    for t, lanes in enumerate(columns):
                        number = (chunk * groups + group) * len(columns) + t
                        value = in_ref[pl.ds(2 * TILE * message_place(number, LINES), TILE), :]
                        stat_ref[rows, lanes] = value
                        total = total + value * value
                        first = 2 * TILE * DEPTH * (LINES * t + group) + TILE + chunk
                        work_ref[rows, lanes] = in_ref[
                            pl.ds(first, TILE, stride=2 * TILE), :
                        ]
        total_ref[...] = total

    def diagonal(first, rows, value):
        row = lax.broadcasted_iota(jnp.int32, (rows, width), 0)
        column = lax.broadcasted_iota(jnp.int32, (rows, width), 1)
        return jnp.where(column == row + first, value, 0.0)

    def each_block(left_ref, right_ref, take):
        for first in range(0, width, step):
            rows = pl.ds(first, step)
            take(first, product(lambda terms: left_ref[rows, pl.ds(0, terms)], right_ref, 3))

    def row_product(rows, right_ref):
        pieces = jnp.concatenate(cut(rows, 2), 1)
        return product(lambda terms: pieces[:, :terms], right_ref, 2)

    @pl.when(core_ref[0] == 0)
    def _():
        assemble(own_ref, other_ref)

    @pl.when(core_ref[0] != 0)
    def _():
        assemble(other_ref, own_ref)

    chosen = []
    for chunk in (y_ref[0], chunks - 1 - y_ref[0]):
        first = pl.multiple_of(share * chunk + half * core_ref[0], half)
        chosen.append(work_ref[pl.ds(first, half), :])
    chosen = jnp.concatenate(chosen, 0)

    for first in range(0, width, LANES):
        value = work_ref[pl.ds(first, LANES), :]
        cut_left(left_ref, 3, first, value)
        cut_right(right_ref, 3, first, value)

    def take_square(first, value):
        cut_left(next_ref, 3, first, value)
        cut_right(square_ref, 3, first, value)

    each_block(left_ref, right_ref, take_square)

    total = jnp.sum(jnp.sum(total_ref[...], axis=0, keepdims=True), axis=1, keepdims=True)
    inverse = 1.0 / jnp.sqrt(total + 1e-06)
    for first in range(0, width, LANES):
        value = stat_ref[pl.ds(first, LANES), :] * inverse + diagonal(first, LANES, DAMPING)
        cut_right(scaled_ref, 3, first, value)
    each_block(next_ref, square_ref, lambda first, value: cut_left(left_ref, 3, first, value))

    def take_coupled(first, value):
        work_ref[pl.ds(first, step), :] = value
        cut_right(right_ref, 2, first, (diagonal(first, step, 5.0) - value) * 0.25)

    each_block(left_ref, scaled_ref, take_coupled)
    factor_ref = right_ref.at[pl.ds(0, 2 * width)]
    estimate = row_product(chosen, factor_ref)
    out_ref[...] = estimate

    @pl.when(count_ref[0] >= 2)
    def _():
        for first in range(0, width, LANES):
            cut_right(square_ref, 2, first, work_ref[pl.ds(first, LANES), :])
        coupled_ref = square_ref.at[pl.ds(0, 2 * width)]
        rows = estimate
        for matrix in (factor_ref, factor_ref, factor_ref, factor_ref, coupled_ref):
            rows = row_product(rows, matrix)
        out_ref[...] = (5.0 * estimate - rows) * 0.25


def newton(core, y, count, own, other, width):
    square = (width, width)
    return pl.pallas_call(
        newton_kernel,
        out_shape=shape_of(width // TILE, width),
        in_specs=[SMEM] * 3 + [VMEM] * 2,
        out_specs=VMEM,
        scratch_shapes=[
            pltpu.VMEM(square, jnp.float32),
            pltpu.VMEM(square, jnp.float32),
            pltpu.VMEM((TILE, LANES), jnp.float32),
            pltpu.VMEM((width, 3 * width), jnp.bfloat16),
            pltpu.VMEM((width, 3 * width), jnp.bfloat16),
            pltpu.VMEM((3 * width, width), jnp.bfloat16),
            pltpu.VMEM((3 * width, width), jnp.bfloat16),
            pltpu.VMEM((3 * width, width), jnp.bfloat16),
        ],
        compiler_params=pltpu.CompilerParams(vmem_limit_bytes=16 * 1024 * 1024),
    )(core, y, count, own, other)


def local(grad, prev_stats, warm_roots, owner_items, counts, read_shard):
    gradients = grad[:, 0]
    width = gradients.shape[-1]
    kinds, lines = lax.axis_size("yh"), lax.axis_size("yl")
    y_count = kinds * lines
    kind = lax.axis_index("yh")
    y = kind * lines + lax.axis_index("yl")
    core = lax.axis_index("core")
    worker = lax.axis_index(WORKER)
    half = width // y_count // 2
    weight = (1.0 - HISTORY) / (y_count * 2 * gradients.shape[0])

    kept, sent = gram_halves(core.reshape(1), gradients, half, weight)
    got = lax.ppermute(sent, "core", SWAP)
    messages = build_messages(y.reshape(1), kept, got, prev_stats[0], warm_roots[0])
    peers = kept.shape[0]
    arrived = lax.all_to_all(messages.reshape(peers, 1, -1), PLANE, 0, 0, tiled=True)

    ids = jnp.arange(read_shard.shape[0], dtype=jnp.int32)
    blocks = jnp.sum(jnp.where(read_shard[None, :] == ids[:, None], ids[None, :], 0), 1)
    items = (2 * blocks[:, None] + jnp.arange(2, dtype=jnp.int32)).reshape(-1)
    matches = owner_items[None] == items[:, None, None]
    owners = jnp.sum(jnp.where(matches, ids[None, :, None], 0), (1, 2))
    slots = jnp.sum(jnp.where(matches, jnp.arange(2, dtype=jnp.int32), 0), (1, 2))
    mine = jnp.arange(counts.shape[0], dtype=jnp.int32) == 2 * blocks[worker] + kind
    iterations = jnp.sum(jnp.where(mine, counts, 0)).reshape(1)

    tiles = deliver(
        kind.reshape(1), blocks, owners, slots, arrived.reshape(messages.shape)
    )
    own = lax.all_to_all(tiles, LINE, 0, 0, tiled=True)
    other = lax.ppermute(own, "core", SWAP)
    root_rows = newton(
        core.reshape(1),
        y.reshape(1),
        iterations,
        own.reshape(-1, LANES),
        other.reshape(-1, LANES),
        width,
    )
    pairs = [(i, y_count - 1 - i) for i in range(y_count)]
    root_kept = root_rows[:half]
    root_got = lax.ppermute(root_rows[half:], ("yh", "yl"), pairs)
    result = jnp.where(
        kind == 0, jnp.stack([root_kept, root_got]), jnp.stack([root_got, root_kept])
    )
    return result[None]


def solution(mesh):
    kinds, cores, x_count = 2, 2, 4
    dp_count, worker_count = mesh.devices.shape
    chips = Mesh(
        mesh.devices.reshape(
            kinds, dp_count // (kinds * cores), cores, x_count, worker_count // x_count
        ),
        ("yh", "yl", "core", "x", "z"),
    )
    dp = ("yh", "yl", "core")
    return jax.shard_map(
        local,
        mesh=chips,
        in_specs=(
            P(dp, WORKER, None, None),
            P(WORKER, None, dp, None),
            P(WORKER, None, dp, None),
            P(),
            P(),
            P(),
        ),
        out_specs=P(WORKER, None, dp, None),
        check_vma=False,
    )
```

```python
import jax
import jax.numpy as jnp
from jax import lax
from jax.experimental import pallas as pl
from jax.experimental.pallas import tpu as pltpu
from jax.sharding import Mesh, PartitionSpec as P

HISTORY = 0.5
DAMPING = 0.001
WORKER = ("x", "z")
PLANE = ("x", "yh", "yl", "z")
LINE = ("x", "yl", "z")
SWAP = [(0, 1), (1, 0)]
LANES = 128
TILE = 8
EXTRA = 2
DEPTH = 8
LINES = 4
SMEM = pl.BlockSpec(memory_space=pltpu.SMEM)
VMEM = pl.BlockSpec(memory_space=pltpu.VMEM)
PARAMS = pltpu.CompilerParams(vmem_limit_bytes=8 * 1024 * 1024)


def shape_of(*shape):
    return jax.ShapeDtypeStruct(shape, jnp.float32)


def tile_columns(width):
    return [pl.ds(LANES * t, LANES) for t in range(width // LANES)]


def halves_kernel(weight, half, core_ref, grad_ref, kept_ref, sent_ref, gram_ref):
    core = core_ref[0]
    terms, width, _ = grad_ref.shape
    groups = half // TILE
    columns = tile_columns(width)
    chunks = width // (2 * half)
    count = chunks * groups * len(columns)
    step = 4 * LANES
    for kind in range(2):
        for first in range(0, width, step):
            part = pl.ds(first, step)
            total = jnp.zeros((step, width), jnp.float32)
            for term in range(terms):
                if kind == 0:
                    rows, axis = grad_ref[term, part, :], 1
                else:
                    rows, axis = grad_ref[term, :, part], 0
                total = total + lax.dot_general(
                    rows,
                    grad_ref[term],
                    (((axis,), (axis,)), ((), ())),
                    preferred_element_type=jnp.float32,
                )
            gram_ref[kind, part, :] = total * weight
    for out_ref, part in ((kept_ref, core), (sent_ref, 1 - core)):
        for kind in range(2):
            for chunk in range(chunks):
                for group in range(groups):
                    first = pl.multiple_of(2 * half * chunk + half * part + TILE * group, TILE)
                    for t, lanes in enumerate(columns):
                        number = (chunk * groups + group) * len(columns) + t + count * kind
                        out_ref[number] = gram_ref[kind, pl.ds(first, TILE), lanes]


def gram_halves(core, gradients, half, weight):
    width = gradients.shape[1]
    messages = width * width // (TILE * LANES)

    def kernel(*refs):
        halves_kernel(weight, half, *refs)

    return pl.pallas_call(
        kernel,
        out_shape=[shape_of(messages, TILE, LANES)] * 2,
        in_specs=[SMEM, VMEM],
        out_specs=[VMEM] * 2,
        scratch_shapes=[pltpu.VMEM((2, width, width), jnp.float32)],
        compiler_params=PARAMS,
    )(core, gradients)


def message_place(number, chunks):
    columns = 4
    chunk, piece = divmod(number, columns * DEPTH)
    return (piece % columns * chunks + chunk) * DEPTH + piece // columns


def message_kernel(y_ref, kept_ref, got_ref, prev_ref, warm_ref, out_ref):
    _, rows, width = warm_ref.shape
    columns = tile_columns(width)
    size = TILE + EXTRA
    for number in range(kept_ref.shape[0]):
        first = size * message_place(number, TILE)
        out_ref[pl.ds(first, TILE), :] = kept_ref[number] + got_ref[number]
    count = kept_ref.shape[0] // 2
    shares = rows // TILE * len(columns)
    for kind in range(2):
        for part in range(shares):
            group, t = divmod(part, len(columns))
            number = count * kind + y_ref[0] * shares + part
            value = HISTORY * prev_ref[kind, pl.ds(TILE * group, TILE), columns[t]]
            line = DEPTH * (2 * LINES * t + LINES * kind) + LINES * y_ref[0] + group
            out_ref[pl.ds(size * line, TILE), :] = kept_ref[number] + got_ref[number] + value
    for kind in range(2):
        for slot in range(EXTRA):
            for t, lanes in enumerate(columns):
                for first in range(0, rows, TILE):
                    line = DEPTH * (2 * LINES * t + LINES * kind + first // TILE)
                    out_ref[
                        pl.ds(size * line + TILE + slot, TILE, stride=size), :
                    ] = warm_ref[slot, pl.ds(first, TILE), lanes]


def build_messages(y, kept, got, prev, warm):
    return pl.pallas_call(
        message_kernel,
        out_shape=shape_of(kept.shape[0] * (TILE + EXTRA), LANES),
        in_specs=[SMEM] + [VMEM] * 4,
        out_specs=VMEM,
        compiler_params=PARAMS,
    )(y, kept, got, prev, warm)


def deliver_kernel(kind_ref, block_ref, owner_ref, slot_ref, in_ref, out_ref, sum_ref, warm_ref):
    kind = kind_ref[0]
    workers = block_ref.shape[0]
    size = TILE + EXTRA
    chunks = in_ref.shape[0] // (workers * size)
    stride = DEPTH * size
    for worker in range(workers):
        base = size * (worker // DEPTH * chunks * DEPTH + worker % DEPTH)
        total = in_ref[pl.ds(base, TILE), :]
        for chunk in range(1, chunks):
            total = total + in_ref[pl.ds(base + stride * chunk, TILE), :]
        sum_ref[worker] = total
        for slot in range(EXTRA):
            first = base + TILE + slot
            warm_ref[EXTRA * worker + slot] = in_ref[pl.ds(first, chunks, stride=stride), :]
    for reader in range(workers):
        place = 2 * reader + kind
        sums = sum_ref[block_ref[reader]]
        warm = warm_ref[EXTRA * owner_ref[place] + slot_ref[place]]
        for line in range(LINES):
            number = (reader // DEPTH * LINES + line) * DEPTH + reader % DEPTH
            out_ref[number, pl.ds(0, TILE), :] = sums
            out_ref[number, pl.ds(TILE, TILE), :] = warm


def deliver(kind, blocks, owners, slots, messages):
    workers = blocks.shape[0]
    rows = messages.shape[0]
    return pl.pallas_call(
        deliver_kernel,
        out_shape=shape_of(rows // (TILE + EXTRA) // 2, 2 * TILE, LANES),
        in_specs=[SMEM] * 4 + [VMEM],
        out_specs=VMEM,
        scratch_shapes=[
            pltpu.VMEM((workers, TILE, LANES), jnp.float32),
            pltpu.VMEM((workers * EXTRA, TILE, LANES), jnp.float32),
        ],
        compiler_params=PARAMS,
    )(kind, blocks, owners, slots, messages)


def cut(value, parts):
    pieces = []
    for number in range(parts):
        piece = value.astype(jnp.bfloat16)
        pieces.append(piece)
        if number < parts - 1:
            value = value - piece.astype(jnp.float32)
    return pieces


def cut_left(out_ref, parts, first, value):
    rows, width = value.shape
    for number, piece in enumerate(cut(value, parts)):
        out_ref[pl.ds(first, rows), pl.ds(width * number, width)] = piece


def cut_right(out_ref, parts, first, value):
    rows, width = value.shape
    for number, piece in enumerate(cut(value, parts)):
        out_ref[pl.ds(width * (parts - 1 - number) + first, rows), :] = piece


def product(left_of, right_ref, parts):
    width = right_ref.shape[1]
    total = None
    for count in reversed(range(1, parts + 1)):
        term = jnp.dot(
            left_of(width * count),
            right_ref[pl.ds(width * (parts - count), width * count), :],
            preferred_element_type=jnp.float32,
        )
        total = term if total is None else total + term
    return total


def newton_kernel(
    core_ref, y_ref, count_ref, own_ref, other_ref, out_ref,
    stat_ref, work_ref, total_ref, left_ref, next_ref, right_ref, square_ref, scaled_ref
):
    width = stat_ref.shape[0]
    columns = tile_columns(width)
    chunks = TILE
    share = width // chunks
    half = share // 2
    groups = half // TILE
    step = 4 * LANES

    def assemble(*halves):
        total = jnp.zeros((TILE, LANES), jnp.float32)
        for part, in_ref in enumerate(halves):
            for chunk in range(chunks):
                for group in range(groups):
                    rows = pl.ds(share * chunk + half * part + TILE * group, TILE)
                    for t, lanes in enumerate(columns):
                        number = (chunk * groups + group) * len(columns) + t
                        value = in_ref[pl.ds(2 * TILE * message_place(number, LINES), TILE), :]
                        stat_ref[rows, lanes] = value
                        total = total + value * value
                        first = 2 * TILE * DEPTH * (LINES * t + group) + TILE + chunk
                        work_ref[rows, lanes] = in_ref[
                            pl.ds(first, TILE, stride=2 * TILE), :
                        ]
        total_ref[...] = total

    def diagonal(first, rows, value):
        row = lax.broadcasted_iota(jnp.int32, (rows, width), 0)
        column = lax.broadcasted_iota(jnp.int32, (rows, width), 1)
        return jnp.where(column == row + first, value, 0.0)

    def each_block(left_ref, right_ref, take):
        for first in range(0, width, step):
            rows = pl.ds(first, step)
            take(first, product(lambda terms: left_ref[rows, pl.ds(0, terms)], right_ref, 3))

    def row_product(rows, right_ref):
        pieces = jnp.concatenate(cut(rows, 2), 1)
        return product(lambda terms: pieces[:, :terms], right_ref, 2)

    @pl.when(core_ref[0] == 0)
    def _():
        assemble(own_ref, other_ref)

    @pl.when(core_ref[0] != 0)
    def _():
        assemble(other_ref, own_ref)

    chosen = []
    for chunk in (y_ref[0], chunks - 1 - y_ref[0]):
        first = pl.multiple_of(share * chunk + half * core_ref[0], half)
        chosen.append(work_ref[pl.ds(first, half), :])
    chosen = jnp.concatenate(chosen, 0)

    for first in range(0, width, LANES):
        value = work_ref[pl.ds(first, LANES), :]
        cut_left(left_ref, 3, first, value)
        cut_right(right_ref, 3, first, value)

    def take_square(first, value):
        cut_left(next_ref, 3, first, value)
        cut_right(square_ref, 3, first, value)

    each_block(left_ref, right_ref, take_square)

    total = jnp.sum(jnp.sum(total_ref[...], axis=0, keepdims=True), axis=1, keepdims=True)
    inverse = 1.0 / jnp.sqrt(total + 1e-06)
    for first in range(0, width, LANES):
        value = stat_ref[pl.ds(first, LANES), :] * inverse + diagonal(first, LANES, DAMPING)
        cut_right(scaled_ref, 3, first, value)
    each_block(next_ref, square_ref, lambda first, value: cut_left(left_ref, 3, first, value))

    def take_coupled(first, value):
        work_ref[pl.ds(first, step), :] = value
        cut_right(right_ref, 2, first, (diagonal(first, step, 5.0) - value) * 0.25)

    each_block(left_ref, scaled_ref, take_coupled)
    factor_ref = right_ref.at[pl.ds(0, 2 * width)]
    estimate = row_product(chosen, factor_ref)
    out_ref[...] = estimate

    @pl.when(count_ref[0] >= 2)
    def _():
        for first in range(0, width, LANES):
            cut_right(square_ref, 2, first, work_ref[pl.ds(first, LANES), :])
        coupled_ref = square_ref.at[pl.ds(0, 2 * width)]
        rows = estimate
        for matrix in (factor_ref, factor_ref, factor_ref, factor_ref, coupled_ref):
            rows = row_product(rows, matrix)
        out_ref[...] = (5.0 * estimate - rows) * 0.25


def newton(core, y, count, own, other, width):
    square = (width, width)
    return pl.pallas_call(
        newton_kernel,
        out_shape=shape_of(width // TILE, width),
        in_specs=[SMEM] * 3 + [VMEM] * 2,
        out_specs=VMEM,
        scratch_shapes=[
            pltpu.VMEM(square, jnp.float32),
            pltpu.VMEM(square, jnp.float32),
            pltpu.VMEM((TILE, LANES), jnp.float32),
            pltpu.VMEM((width, 3 * width), jnp.bfloat16),
            pltpu.VMEM((width, 3 * width), jnp.bfloat16),
            pltpu.VMEM((3 * width, width), jnp.bfloat16),
            pltpu.VMEM((3 * width, width), jnp.bfloat16),
            pltpu.VMEM((3 * width, width), jnp.bfloat16),
        ],
        compiler_params=pltpu.CompilerParams(vmem_limit_bytes=16 * 1024 * 1024),
    )(core, y, count, own, other)


def local(grad, prev_stats, warm_roots, owner_items, counts, read_shard):
    gradients = grad[:, 0]
    width = gradients.shape[-1]
    kinds, lines = lax.axis_size("yh"), lax.axis_size("yl")
    y_count = kinds * lines
    kind = lax.axis_index("yh")
    y = kind * lines + lax.axis_index("yl")
    core = lax.axis_index("core")
    worker = lax.axis_index(WORKER)
    half = width // y_count // 2
    weight = (1.0 - HISTORY) / (y_count * 2 * gradients.shape[0])

    kept, sent = gram_halves(core.reshape(1), gradients, half, weight)
    got = lax.ppermute(sent, "core", SWAP)
    messages = build_messages(y.reshape(1), kept, got, prev_stats[0], warm_roots[0])
    peers = kept.shape[0]
    arrived = lax.all_to_all(messages.reshape(peers, 1, -1), PLANE, 0, 0, tiled=True)

    ids = jnp.arange(read_shard.shape[0], dtype=jnp.int32)
    blocks = jnp.sum(jnp.where(read_shard[None, :] == ids[:, None], ids[None, :], 0), 1)
    items = (2 * blocks[:, None] + jnp.arange(2, dtype=jnp.int32)).reshape(-1)
    matches = owner_items[None] == items[:, None, None]
    owners = jnp.sum(jnp.where(matches, ids[None, :, None], 0), (1, 2))
    slots = jnp.sum(jnp.where(matches, jnp.arange(2, dtype=jnp.int32), 0), (1, 2))
    mine = jnp.arange(counts.shape[0], dtype=jnp.int32) == 2 * blocks[worker] + kind
    iterations = jnp.sum(jnp.where(mine, counts, 0)).reshape(1)

    tiles = deliver(
        kind.reshape(1), blocks, owners, slots, arrived.reshape(messages.shape)
    )
    own = lax.all_to_all(tiles, LINE, 0, 0, tiled=True)
    other = lax.ppermute(own, "core", SWAP)
    root_rows = newton(
        core.reshape(1),
        y.reshape(1),
        iterations,
        own.reshape(-1, LANES),
        other.reshape(-1, LANES),
        width,
    )
    pairs = [(i, y_count - 1 - i) for i in range(y_count)]
    root_kept = root_rows[:half]
    root_got = lax.ppermute(root_rows[half:], ("yh", "yl"), pairs)
    result = jnp.where(
        kind == 0, jnp.stack([root_kept, root_got]), jnp.stack([root_got, root_kept])
    )
    return result[None]


def solution(mesh):
    kinds, cores, x_count = 2, 2, 4
    dp_count, worker_count = mesh.devices.shape
    chips = Mesh(
        mesh.devices.reshape(
            kinds, dp_count // (kinds * cores), cores, x_count, worker_count // x_count
        ),
        ("yh", "yl", "core", "x", "z"),
    )
    dp = ("yh", "yl", "core")
    return jax.shard_map(
        local,
        mesh=chips,
        in_specs=(
            P(dp, WORKER, None, None),
            P(WORKER, None, dp, None),
            P(WORKER, None, dp, None),
            P(),
            P(),
            P(),
        ),
        out_specs=P(WORKER, None, dp, None),
        check_vma=False,
    )
```
